256 devices in a mesh: row: 128 (over z_lo, y, x, core), pair: 2 (over z_hi).
Axes of the slice: x: 4, y: 4, z: 8 (z_hi: 2, z_lo: 4; z = z_hi * 4 + z_lo), core: 2. Of those that a mesh axis runs over, the one named last changes fastest.
Arguments:
- slab: float32 [524288, 512], P('row', 'pair'), may hold values from -260 to 260, as said below
- block_ids: int32 [4], P('pair'), may hold values from 0 to 3, each once
Outputs:
- new_slab: float32 [524288, 512], P('row', 'pair')
- col_norms: float32 [512], P('pair')
- new_ids: int32 [4], P('pair')
The draws below stay inside these ranges and needn't reach their ends.
Inputs may be any that keep to these rules, and one draw needn't show every extreme that they name: `slab`: finite values; within each pair the columns have distinct scales.
All inputs are finite; a program needn't handle non-finite values.
Results may differ from the reference program's by a relative error of at most 0.0003.
Values sent between devices are 32-bit elements; how exact they have to be, the bound alone decides.
No kernel may reach another device: no remote copies, remote signals or barrier semaphores. Data moves between devices by JAX's collectives and lax.ppermute only.
A program may use at most 64 MiB of HBM per device.

```python
import jax
import jax.numpy as jnp
import numpy as np
from jax import lax

BLOCK = 128
ROUNDS = 48
ROWS = 524288
COL_BLOCKS = 4
COLS = 512


def draw_slab(key, part):
    key = jax.random.fold_in(key, 11)
    width = 2 * BLOCK
    pairs = COLS // width
    key_rank, key_noise, key_common, key_mix = jax.random.split(key, 4)
    ranks = jax.vmap(lambda sub: jax.random.permutation(sub, width))(jax.random.split(key_rank, pairs))
    col_scale = 1.01 ** ranks.reshape(COLS).astype(jnp.float32)
    row_scale = 1.0 + 0.75 * jnp.arange(ROWS, dtype=jnp.float32) / ROWS
    noise = jnp.clip(jax.random.normal(key_noise, (ROWS, COLS), jnp.float32), -6.0, 6.0)
    common = jnp.clip(jax.random.normal(key_common, (ROWS, 1), jnp.float32), -6.0, 6.0)
    mixing = jnp.clip(jax.random.normal(key_mix, (1, COLS), jnp.float32), -6.0, 6.0)
    values = row_scale[:, None] * col_scale[None, :] * (noise + 0.15 * common * mixing)
    return values.astype(jnp.float32)


def setup_inputs(seed: int = 0) -> dict:
    arg_keys = jax.random.split(jax.random.key(seed), 3)
    return {
        "slab": draw_slab(jax.random.fold_in(arg_keys[2], 71), 0),
        "block_ids": jax.random.permutation(arg_keys[1], COL_BLOCKS).astype(jnp.int32),
    }


def cyclic_tables(width, count):
    partner = np.zeros((count, width), np.int32)
    first_flag = np.zeros((count, width), np.int32)
    for step in range(count):
        for k in range(width // 2):
            if k == 0:
                first, second = (step, width - 1)
            else:
                first, second = ((step + k) % (width - 1), (step - k) % (width - 1))
            partner[step, first] = second
            partner[step, second] = first
            first_flag[step, first] = 1
    return (jnp.asarray(partner), jnp.asarray(first_flag))

def jacobi_rounds(gram, count):
    width = gram.shape[0]
    partner_tab, first_tab = cyclic_tables(width, count)
    columns = lax.broadcasted_iota(jnp.int32, (width, width), 1)
    rows_iota = lax.broadcasted_iota(jnp.int32, (width, width), 0)
    on_diag = rows_iota == columns

    def one_round(step, state):
        mat, rot = state
        partner = partner_tab[step]
        is_first = first_tab[step] > 0
        pick = partner[:, None] == columns
        picked = jnp.where(pick, mat, jnp.zeros_like(mat))
        diag = jnp.diagonal(mat)
        row_part = lax.optimization_barrier(jnp.sum(picked, axis=1))
        col_part = lax.optimization_barrier(jnp.sum(picked, axis=0))
        other = lax.optimization_barrier(jnp.sum(jnp.where(pick, diag[None, :], jnp.zeros_like(mat)), axis=1))
        gpq = jnp.where(is_first, row_part, col_part)
        gpp = jnp.where(is_first, diag, other)
        gqq = jnp.where(is_first, other, diag)
        diff = gqq - gpp
        sgn = jnp.where(diff >= 0, 1.0, -1.0).astype(mat.dtype)
        den = jnp.abs(diff) + jnp.sqrt(diff * diff + 4.0 * gpq * gpq)
        tang = jnp.where(den > 0, 2.0 * gpq * sgn / jnp.where(den > 0, den, 1.0), 0.0)
        cosv = 1.0 / jnp.sqrt(1.0 + tang * tang)
        sinv = tang * cosv
        offset = jnp.where(is_first, -sinv, sinv)
        rotation = jnp.where(on_diag, cosv[None, :], jnp.where(pick, offset[None, :], jnp.zeros_like(mat)))
        left = jnp.dot(rotation.T, mat, precision=lax.Precision.HIGHEST, preferred_element_type=mat.dtype)
        mat = jnp.dot(left, rotation, precision=lax.Precision.HIGHEST, preferred_element_type=mat.dtype)
        rot = jnp.dot(rot, rotation, precision=lax.Precision.HIGHEST, preferred_element_type=mat.dtype)
        return (mat, rot)
    start = (gram, jnp.eye(width, dtype=gram.dtype))
    return lax.fori_loop(0, count, one_round, start)

def reference(slab, block_ids):
    width = 2 * BLOCK
    pairs = COLS // width
    cube = slab.reshape(ROWS, pairs, width).transpose(1, 0, 2)

    def per_pair(piece):
        gram = lax.dot_general(piece, piece, (((0,), (0,)), ((), ())), precision=lax.Precision.HIGHEST, preferred_element_type=jnp.float32)
        gram, rot = jacobi_rounds(gram, ROUNDS)
        return jnp.dot(piece, rot, precision=lax.Precision.HIGHEST, preferred_element_type=jnp.float32)
    rotated = lax.map(per_pair, cube)
    labels = block_ids.reshape(pairs, 2)
    second_leaves = labels[:, 1] > labels[:, 0]
    first = rotated[:, :, :BLOCK]
    second = rotated[:, :, BLOCK:]
    staying = jnp.where(second_leaves[:, None, None], first, second)
    leaving = jnp.where(second_leaves[:, None, None], second, first)
    arrived = jnp.roll(leaving, 1, axis=0)
    new_slab = jnp.concatenate([staying, arrived], axis=2).transpose(1, 0, 2).reshape(ROWS, COLS)
    col_norms = jnp.sqrt(lax.optimization_barrier(jnp.sum(new_slab * new_slab, axis=0)) / ROWS)
    stay_label = jnp.where(second_leaves, labels[:, 0], labels[:, 1])
    leave_label = jnp.where(second_leaves, labels[:, 1], labels[:, 0])
    new_ids = jnp.stack([stay_label, jnp.roll(leave_label, 1)], axis=1).reshape(COL_BLOCKS).astype(jnp.int32)
    return (new_slab, col_norms, new_ids)
```

```python
import functools

import jax
import jax.numpy as jnp
from jax import lax
from jax.experimental import pallas as pl
from jax.experimental.pallas import tpu as pltpu
from jax.sharding import PartitionSpec as P

ROUNDS = 48
BLOCK = 128
WIDTH = 256
F32 = jnp.float32
BF16 = jnp.bfloat16
HIGHEST = lax.Precision.HIGHEST
VMEM_LIMIT = 32 * 1024 * 1024


def product(a, b):
    return jnp.dot(a, b, preferred_element_type=F32)


def product_over_rows(a, b):
    return lax.dot_general(a, b, (((0,), (0,)), ((), ())), preferred_element_type=F32)


def gram_kernel(x_ref, out_ref, even, odd):
    step = pl.program_id(0)

    @pl.when(step == 0)
    def _():
        even[...] = jnp.zeros_like(even)
        odd[...] = jnp.zeros_like(odd)

    x = x_ref[...]
    high = x.astype(BF16)
    rest = x - high.astype(F32)
    mid = rest.astype(BF16)
    low = (rest - mid.astype(F32)).astype(BF16)
    even[...] += product_over_rows(high, high) + product_over_rows(mid, mid)
    odd[...] += product_over_rows(high, mid) + product_over_rows(high, low)

    @pl.when(step == pl.num_programs(0) - 1)
    def _():
        gram = even[...] + odd[...] + odd[...].T
        out_ref[0:128, :] = gram[0:128, 0:128]
        out_ref[128:256, :] = gram[0:128, 128:256]
        out_ref[256:384, :] = gram[128:256, 128:256]


def local_gram(slab, rows=1024):
    return pl.pallas_call(
        gram_kernel,
        grid=(slab.shape[0] // rows,),
        in_specs=[pl.BlockSpec((rows, WIDTH), lambda i: (i, 0))],
        out_specs=pl.BlockSpec((3 * BLOCK, BLOCK), lambda i: (0, 0)),
        out_shape=jax.ShapeDtypeStruct((3 * BLOCK, BLOCK), F32),
        scratch_shapes=[pltpu.VMEM((WIDTH, WIDTH), F32), pltpu.VMEM((WIDTH, WIDTH), F32)],
        compiler_params=pltpu.CompilerParams(vmem_limit_bytes=VMEM_LIMIT),
    )(slab)


def exchanged(array, mask):
    return lax.ppermute(array, "row", [(i, i ^ mask) for i in range(128)])


def row_part(array, index, rows):
    return lax.dynamic_slice_in_dim(array, index * rows, rows, 0)


def summed_over_four(mine, shift):
    got = [exchanged(mine, d << shift) for d in (1, 2, 3)]
    return (mine + got[1]) + (got[0] + got[2])


def summed_over_rows(part):
    me = lax.axis_index("row")
    core, x = me & 1, (me >> 1) & 3
    half = part.shape[0] // 2
    quarter = half // 4
    total = row_part(part, core, half) + exchanged(row_part(part, 1 - core, half), 1)
    got = [exchanged(row_part(total, x ^ d, quarter), d << 1) for d in (1, 2, 3)]
    total = (row_part(total, x, quarter) + got[1]) + (got[0] + got[2])
    total = summed_over_four(total, 3)
    total = summed_over_four(total, 5)
    parts = jnp.stack([total] + [exchanged(total, d << 1) for d in (1, 2, 3)])
    total = jnp.concatenate([lax.dynamic_index_in_dim(parts, x ^ j, 0, False) for j in range(4)])
    other = exchanged(total, 1)
    return jnp.where(
        core == 0, jnp.concatenate([total, other]), jnp.concatenate([other, total])
    )


def angles(g, d_top, d_bot):
    diff = d_bot - d_top
    sgn = jnp.where(diff >= 0, 1.0, -1.0)
    den = jnp.abs(diff) + jnp.sqrt(diff * diff + 4.0 * g * g)
    tang = jnp.where(den > 0, 2.0 * g * sgn / jnp.where(den > 0, den, 1.0), 0.0)
    cosv = 1.0 / jnp.sqrt(1.0 + tang * tang)
    return tang, cosv, tang * cosv

def jacobi_kernel(rounds, swap_ref, gram_ref, leave_ref, stay_ref, diag_ref, vt, vb, wt, wb):
    half = 128
    lane = lax.broadcasted_iota(jnp.int32, (8, half), 1)
    first, last = lane == 0, lane == half - 1
    row = lax.broadcasted_iota(jnp.int32, (2 * half, half), 0)
    col = lax.broadcasted_iota(jnp.int32, (2 * half, half), 1)
    vt[...] = (row == col).astype(F32)
    vb[...] = (row == 255 - col).astype(F32)
    a, b, c = gram_ref[0:128, :], gram_ref[128:256, :], gram_ref[256:384, :]
    rev = (row[:half] == half - 1 - col[:half]).astype(F32)
    wt[0:128, :] = a
    wt[128:256, :] = b.T
    wb[0:128, :] = jnp.dot(b, rev, precision=HIGHEST, preferred_element_type=F32)
    wb[128:256, :] = jnp.dot(c, rev, precision=HIGHEST, preferred_element_type=F32)
    eye = row[:half] == col[:half]
    d_top = jnp.sum(jnp.where(eye, wt[0:128, :], 0.0), axis=0, keepdims=True)
    anti = row[:half] == half - 1 - col[:half]
    d_bot = jnp.sum(jnp.where(anti, wb[128:256, :], 0.0), axis=0, keepdims=True)
    g = (jnp.sum(jnp.where(eye, wb[0:128, :], 0.0), axis=0, keepdims=True))
    d_top, d_bot, g = (jnp.broadcast_to(v, (8, half)) for v in (d_top, d_bot, g))

    def shifted(top, bot):
        new_top = jnp.where(last, bot, pltpu.roll(top, half - 1, 1))
        new_bot = jnp.where(first, bot, pltpu.roll(jnp.where(first, top, bot), 1, 1))
        return new_top, new_bot

    def one_round(_, state):
        g, d_top, d_bot = state
        t, c, s = angles(g, d_top, d_bot)
        d_top, d_bot = shifted(d_top - t * g, d_bot + t * g)
        acc = [jnp.zeros((8, half), F32) for _ in range(4)]
        for k in range(32):
            sl = pl.ds(8 * k, 8)
            a, b = vt[sl, :], vb[sl, :]
            nvt, nvb = shifted(c * a - s * b, s * a + c * b)
            vt[sl, :] = nvt
            vb[sl, :] = nvb
            a, b = wt[sl, :], wb[sl, :]
            nwt, nwb = shifted(c * a - s * b, s * a + c * b)
            wt[sl, :] = nwt
            wb[sl, :] = nwb
            acc[k % 4] = acc[k % 4] + nvt * nwb
        g = jnp.sum((acc[0] + acc[1]) + (acc[2] + acc[3]), axis=0, keepdims=True)
        return jnp.broadcast_to(g, (8, half)), d_top, d_bot

    g, d_top, d_bot = lax.fori_loop(0, rounds, one_round, (g, d_top, d_bot))
    swap = swap_ref[0]
    r = lax.broadcasted_iota(jnp.int32, (half, 2 * half), 0)
    j = lax.broadcasted_iota(jnp.int32, (half, 2 * half), 1)
    idx = jnp.where(swap > 0, jnp.where(j >= half, j - half, j + half), j)
    p_top = (r + rounds == idx).astype(F32)
    back = rounds - idx
    back = jnp.where(idx == 2 * half - 1, 0, jnp.where(back <= 0, back + 255, back))
    p_bot = ((r == back) & ((idx < rounds) | (idx >= rounds + half))).astype(F32)
    dot = functools.partial(jnp.dot, precision=HIGHEST, preferred_element_type=F32)
    rot = dot(vt[...], p_top) + dot(vb[...], p_bot)
    high = rot.astype(BF16)
    low = (rot - high.astype(F32)).astype(BF16)
    stay_ref[:, 0:128] = high[:, 0:128]
    stay_ref[:, 128:256] = low[:, 0:128]
    leave_ref[:, 0:128] = high[:, 128:256]
    leave_ref[:, 128:256] = low[:, 128:256]
    diag_ref[...] = dot(d_top, p_top) + dot(d_bot, p_bot)

def jacobi(gram, swap):
    in_vmem = pl.BlockSpec(memory_space=pltpu.VMEM)
    return pl.pallas_call(
        functools.partial(jacobi_kernel, ROUNDS),
        in_specs=[pl.BlockSpec(memory_space=pltpu.SMEM), in_vmem],
        out_specs=(in_vmem, in_vmem, in_vmem),
        out_shape=(
            jax.ShapeDtypeStruct((WIDTH, WIDTH), BF16),
            jax.ShapeDtypeStruct((WIDTH, WIDTH), BF16),
            jax.ShapeDtypeStruct((8, WIDTH), F32),
        ),
        scratch_shapes=[pltpu.VMEM((WIDTH, BLOCK), F32)] * 4,
        compiler_params=pltpu.CompilerParams(vmem_limit_bytes=VMEM_LIMIT),
    )(swap, gram)


def rotate_kernel(x_ref, rot_ref, out_ref):
    x = x_ref[...]
    high = x.astype(BF16)
    low = (x - high.astype(F32)).astype(BF16)
    both = product(high, rot_ref[...])
    out_ref[...] = (both[:, 0:128] + both[:, 128:256]) + product(low, rot_ref[:, 0:128])


def rotated(slab, rot, columns, rows=1024):
    count = slab.shape[0]
    return pl.pallas_call(
        rotate_kernel,
        grid=(count // rows,),
        in_specs=[
            pl.BlockSpec((rows, WIDTH), lambda i: (i, 0)),
            pl.BlockSpec((WIDTH, WIDTH), lambda i: (0, 0)),
        ],
        out_specs=pl.BlockSpec((rows, BLOCK), lambda i: (i, 0)),
        out_shape=jax.ShapeDtypeStruct((count, columns), F32),
        compiler_params=pltpu.CompilerParams(vmem_limit_bytes=VMEM_LIMIT),
        cost_estimate=pl.CostEstimate(
            flops=6 * count * WIDTH * BLOCK, bytes_accessed=6 * count * WIDTH, transcendentals=0
        ),
    )(slab, rot)


def passed_along(array):
    return lax.ppermute(array, "pair", [(0, 1), (1, 0)])


def per_device(slab, block_ids):
    swap = (block_ids[1] <= block_ids[0]).astype(jnp.int32)
    stay_label = jnp.where(swap > 0, block_ids[1], block_ids[0])
    leave_label = jnp.where(swap > 0, block_ids[0], block_ids[1])
    gram = summed_over_rows(local_gram(slab))
    rot_leave, rot_stay, diag = jacobi(gram, swap.reshape(1))
    diag = diag[0]
    note = jnp.concatenate([diag[BLOCK:], jnp.full((BLOCK,), leave_label.astype(F32))])
    note = passed_along(note)
    leaving, note = lax.optimization_barrier((rotated(slab, rot_leave, BLOCK), note))
    arrived = passed_along(leaving)
    new_slab = rotated(slab, rot_stay, WIDTH)
    new_slab = lax.dynamic_update_slice(new_slab, arrived, (0, BLOCK))
    total_rows = slab.shape[0] * lax.axis_size("row")
    squares = jnp.concatenate([diag[:BLOCK], note[:BLOCK]])
    col_norms = jnp.sqrt(jnp.maximum(squares, 0.0) / total_rows)
    new_ids = jnp.stack([stay_label, note[BLOCK].astype(jnp.int32)])
    return (new_slab, col_norms, new_ids)


def solution(mesh):
    return jax.shard_map(
        per_device,
        mesh=mesh,
        in_specs=(P("row", "pair"), P("pair")),
        out_specs=(P("row", "pair"), P("pair"), P("pair")),
        check_vma=False,
    )
```

```python
import functools

import jax
import jax.numpy as jnp
from jax import lax
from jax.experimental import pallas as pl
from jax.experimental.pallas import tpu as pltpu
from jax.sharding import PartitionSpec as P

ROUNDS = 48
BLOCK = 128
WIDTH = 256
F32 = jnp.float32
BF16 = jnp.bfloat16
HIGHEST = lax.Precision.HIGHEST
VMEM_LIMIT = 32 * 1024 * 1024
ROWS = 4096
RAW = 640
CHUNKS = (1024, 1792, ROWS - RAW - 2816)
EXTRA = 80
STEP = 128
PACKED = 272
PARTS = 4


def product(a, b):
    return jnp.dot(a, b, preferred_element_type=F32)


def product_over_rows(a, b):
    return lax.dot_general(a, b, (((0,), (0,)), ((), ())), preferred_element_type=F32)


def gram_kernel(slab_ref, out_ref, x_ref, even, odd, sems):
    rows = ROWS // PARTS
    parts = [pl.ds(n * rows, rows) for n in range(PARTS)]
    copies = [
        pltpu.make_async_copy(slab_ref.at[part, :], x_ref.at[part, :], sems.at[n])
        for n, part in enumerate(parts)
    ]
    for copy in copies:
        copy.start()
    for n, part in enumerate(parts):
        copies[n].wait()
        x = x_ref[part, :]
        high = x.astype(BF16)
        rest = x - high.astype(F32)
        mid = rest.astype(BF16)
        low = (rest - mid.astype(F32)).astype(BF16)
        same = product_over_rows(high, high) + product_over_rows(mid, mid)
        cross = product_over_rows(high, mid) + product_over_rows(high, low)
        even[...] = same if n == 0 else even[...] + same
        odd[...] = cross if n == 0 else odd[...] + cross
    gram = even[...] + odd[...] + odd[...].T
    row = lax.broadcasted_iota(jnp.int32, (BLOCK, BLOCK), 0)
    col = lax.broadcasted_iota(jnp.int32, (BLOCK, BLOCK), 1)
    last = gram[128:256, 128:256]
    out_ref[0:128, :] = jnp.where(row <= col, gram[0:128, 0:128], last)
    out_ref[128:256, :] = gram[0:128, 128:256]
    diag = jnp.sum(jnp.where(row == col, last, 0.0), axis=0, keepdims=True)
    out_ref[256:272, :] = jnp.broadcast_to(diag, (16, BLOCK))


def local_gram(slab):
    return pl.pallas_call(
        gram_kernel,
        in_specs=[pl.BlockSpec(memory_space=pl.ANY)],
        out_specs=pl.BlockSpec(memory_space=pltpu.VMEM),
        out_shape=jax.ShapeDtypeStruct((PACKED, BLOCK), F32),
        scratch_shapes=[
            pltpu.VMEM((ROWS, WIDTH), F32),
            pltpu.VMEM((WIDTH, WIDTH), F32),
            pltpu.VMEM((WIDTH, WIDTH), F32),
            pltpu.SemaphoreType.DMA((PARTS,)),
        ],
        compiler_params=pltpu.CompilerParams(vmem_limit_bytes=VMEM_LIMIT),
    )(pltpu.with_memory_space_constraint(slab, pltpu.HBM))


def place():
    me = lax.axis_index("row")
    return me & 1, (me >> 1) & 3


def exchanged(array, mask):
    return lax.ppermute(array, "row", [(i, i ^ mask) for i in range(128)])


def passed_along(array):
    return lax.ppermute(array, "pair", [(0, 1), (1, 0)])


def with_three_others(mine, shift):
    return [mine] + [exchanged(mine, d << shift) for d in (1, 2, 3)]


def summed_over_four(mine, shift):
    parts = with_three_others(mine, shift)
    return (parts[0] + parts[2]) + (parts[1] + parts[3])


def summed_over_rows(part, core, raw):
    half = part.shape[0] // 2
    mine = lax.dynamic_slice_in_dim(part, core * half, half, 0)
    yours = lax.dynamic_slice_in_dim(part, (1 - core) * half, half, 0)
    total = summed_over_four(mine + exchanged(yours, 1), 5)
    raw, total = lax.optimization_barrier((raw, total))
    raw_arrived = passed_along(raw)
    total = summed_over_four(summed_over_four(total, 1), 3)
    return (total, exchanged(total, 1)), raw_arrived


def angles(g, d_top, d_bot):
    diff = d_bot - d_top
    sgn = jnp.where(diff >= 0, 1.0, -1.0)
    den = jnp.abs(diff) + jnp.sqrt(diff * diff + 4.0 * g * g)
    tang = jnp.where(den > 0, 2.0 * g * sgn / jnp.where(den > 0, den, 1.0), 0.0)
    cosv = 1.0 / jnp.sqrt(1.0 + tang * tang)
    return tang, cosv, tang * cosv

def rounds_kernel(
    ids_ref, mine_ref, other_ref, slab_ref, first_ref, second_ref, third_ref, stay_ref, diag_ref,
    packed, vt, vb, wt, wb, leave, x_ref, sem,
):
    rounds = ROUNDS
    fetch = pltpu.make_async_copy(slab_ref.at[pl.ds(RAW, ROWS - RAW), :], x_ref, sem)
    fetch.start()
    core, x = place()
    swap = (ids_ref[1] <= ids_ref[0]).astype(jnp.int32)
    for h, part in enumerate((mine_ref, other_ref)):
        start = pl.multiple_of((core ^ h) * (PACKED // 2), 8)
        packed[pl.ds(start, PACKED // 2), :] = part[...]
    half = 128
    lane = lax.broadcasted_iota(jnp.int32, (8, half), 1)
    first, last = lane == 0, lane == half - 1
    row = lax.broadcasted_iota(jnp.int32, (2 * half, half), 0)
    col = lax.broadcasted_iota(jnp.int32, (2 * half, half), 1)
    vt[...] = (row == col).astype(F32)
    vb[...] = (row == 255 - col).astype(F32)
    both, b = packed[0:128, :], packed[128:256, :]
    mirrored = both.T
    above, below = row[:half] < col[:half], row[:half] > col[:half]
    a = jnp.where(below, mirrored, both)
    c = jnp.where(below, both, jnp.where(above, mirrored, packed[256:257, :]))
    rev = (row[:half] == half - 1 - col[:half]).astype(F32)
    wt[0:128, :] = a
    wt[128:256, :] = b.T
    wb[0:128, :] = jnp.dot(b, rev, precision=HIGHEST, preferred_element_type=F32)
    wb[128:256, :] = jnp.dot(c, rev, precision=HIGHEST, preferred_element_type=F32)
    eye = row[:half] == col[:half]
    d_top = jnp.sum(jnp.where(eye, wt[0:128, :], 0.0), axis=0, keepdims=True)
    anti = row[:half] == half - 1 - col[:half]
    d_bot = jnp.sum(jnp.where(anti, wb[128:256, :], 0.0), axis=0, keepdims=True)
    g = (jnp.sum(jnp.where(eye, wb[0:128, :], 0.0), axis=0, keepdims=True))
    d_top, d_bot, g = (jnp.broadcast_to(v, (8, half)) for v in (d_top, d_bot, g))

    def shifted(top, bot):
        new_top = jnp.where(last, bot, pltpu.roll(top, half - 1, 1))
        new_bot = jnp.where(first, bot, pltpu.roll(jnp.where(first, top, bot), 1, 1))
        return new_top, new_bot

    def one_round(_, state):
        g, d_top, d_bot = state
        t, c, s = angles(g, d_top, d_bot)
        d_top, d_bot = shifted(d_top - t * g, d_bot + t * g)
        acc = [jnp.zeros((8, half), F32) for _ in range(4)]
        for k in range(32):
            sl = pl.ds(8 * k, 8)
            a, b = vt[sl, :], vb[sl, :]
            nvt, nvb = shifted(c * a - s * b, s * a + c * b)
            vt[sl, :] = nvt
            vb[sl, :] = nvb
            a, b = wt[sl, :], wb[sl, :]
            nwt, nwb = shifted(c * a - s * b, s * a + c * b)
            wt[sl, :] = nwt
            wb[sl, :] = nwb
            acc[k % 4] = acc[k % 4] + nvt * nwb
        g = jnp.sum((acc[0] + acc[1]) + (acc[2] + acc[3]), axis=0, keepdims=True)
        return jnp.broadcast_to(g, (8, half)), d_top, d_bot

    g, d_top, d_bot = lax.fori_loop(0, rounds, one_round, (g, d_top, d_bot))
    r = lax.broadcasted_iota(jnp.int32, (half, 2 * half), 0)
    j = lax.broadcasted_iota(jnp.int32, (half, 2 * half), 1)
    idx = jnp.where(swap > 0, jnp.where(j >= half, j - half, j + half), j)
    p_top = (r + rounds == idx).astype(F32)
    back = rounds - idx
    back = jnp.where(idx == 2 * half - 1, 0, jnp.where(back <= 0, back + 255, back))
    p_bot = ((r == back) & ((idx < rounds) | (idx >= rounds + half))).astype(F32)
    dot = functools.partial(jnp.dot, precision=HIGHEST, preferred_element_type=F32)
    rot = dot(vt[...], p_top) + dot(vb[...], p_bot)
    high = rot.astype(BF16)
    low = (rot - high.astype(F32)).astype(BF16)
    stay_ref[:, 0:128] = high[:, 0:128]
    stay_ref[:, 128:256] = low[:, 0:128]
    leave[:, 0:128] = high[:, 128:256]
    leave[:, 128:256] = low[:, 128:256]
    diag = dot(d_top, p_top) + dot(d_bot, p_bot)
    diag_ref[...] = diag
    wt[...] = rot[:, 128:256]
    first_ref[CHUNKS[0] : CHUNKS[0] + 64, :] = wt[pl.ds(pl.multiple_of(x * 64, 64), 64), :]
    first_ref[CHUNKS[0] + 64 : CHUNKS[0] + 72, :] = diag[:, 128:256]
    first_ref[CHUNKS[0] + 72 : CHUNKS[0] + 80, :] = jnp.full((8, half), jnp.maximum(ids_ref[0], ids_ref[1]).astype(F32))
    fetch.wait()
    for n, out_ref in enumerate((first_ref, second_ref, third_ref)):
        base = sum(CHUNKS[:n])

        def one_step(k, _, out_ref=out_ref, base=base):
            start = pl.multiple_of(k * STEP, STEP)
            out_ref[pl.ds(start, STEP), :] = rotation(x_ref[pl.ds(base + start, STEP), :], leave[...])
            return 0

        lax.fori_loop(0, CHUNKS[n] // STEP, one_step, 0, unroll=2)


def rotation(x, rot):
    high = x.astype(BF16)
    low = (x - high.astype(F32)).astype(BF16)
    both = product(high, rot)
    return (both[:, 0:128] + both[:, 128:256]) + product(low, rot[:, 0:128])


def rounds_and_leaving(parts, slab, block_ids):
    in_vmem = pl.BlockSpec(memory_space=pltpu.VMEM)
    return pl.pallas_call(
        rounds_kernel,
        in_specs=[
            pl.BlockSpec(memory_space=pltpu.SMEM),
            in_vmem,
            in_vmem,
            pl.BlockSpec(memory_space=pl.ANY),
        ],
        out_specs=(in_vmem,) * 5,
        out_shape=(
            jax.ShapeDtypeStruct((CHUNKS[0] + EXTRA, BLOCK), F32),
            jax.ShapeDtypeStruct((CHUNKS[1], BLOCK), F32),
            jax.ShapeDtypeStruct((CHUNKS[2], BLOCK), F32),
            jax.ShapeDtypeStruct((WIDTH, WIDTH), BF16),
            jax.ShapeDtypeStruct((8, WIDTH), F32),
        ),
        scratch_shapes=[pltpu.VMEM((PACKED, BLOCK), F32)]
        + [pltpu.VMEM((WIDTH, BLOCK), F32)] * 4
        + [
            pltpu.VMEM((WIDTH, WIDTH), BF16),
            pltpu.VMEM((ROWS - RAW, WIDTH), F32),
            pltpu.SemaphoreType.DMA,
        ],
        compiler_params=pltpu.CompilerParams(vmem_limit_bytes=VMEM_LIMIT),
        cost_estimate=pl.CostEstimate(flops=10**9, bytes_accessed=6 * 2**20, transcendentals=0),
    )(block_ids, *parts, pltpu.with_memory_space_constraint(slab, pltpu.HBM))


def cost(count):
    return pl.CostEstimate(
        flops=6 * count * WIDTH * BLOCK, bytes_accessed=6 * count * WIDTH, transcendentals=0
    )


def staying_kernel(x_ref, rot_ref, out_ref):
    out_ref[...] = rotation(x_ref[...], rot_ref[...])


def staying(slab, rot, rows=512):
    count = slab.shape[0]
    return pl.pallas_call(
        staying_kernel,
        grid=(count // rows,),
        in_specs=[
            pl.BlockSpec((rows, WIDTH), lambda i: (i, 0)),
            pl.BlockSpec((WIDTH, WIDTH), lambda i: (0, 0)),
        ],
        out_specs=pl.BlockSpec((rows, BLOCK), lambda i: (i, 0)),
        out_shape=pltpu.HBM((count, WIDTH), F32),
        compiler_params=pltpu.CompilerParams(vmem_limit_bytes=VMEM_LIMIT),
        cost_estimate=cost(count),
    )(pltpu.with_memory_space_constraint(slab, pltpu.HBM), rot)


def raw_kernel(x_ref, p0_ref, p1_ref, p2_ref, p3_ref, _, out_ref, full, rot):
    @pl.when(pl.program_id(0) == 0)
    def _():
        for d, piece in enumerate((p0_ref, p1_ref, p2_ref, p3_ref)):
            start = (place()[1] ^ d) * 64
            full[pl.ds(pl.multiple_of(start, 64), 64), :] = piece[...]
        high = full[...].astype(BF16)
        rot[:, 0:128] = high
        rot[:, 128:256] = (full[...] - high.astype(F32)).astype(BF16)

    out_ref[...] = rotation(x_ref[...], rot[...])


def rotated_raw(raw, pieces, result, rows=128):
    count = raw.shape[0]
    piece = pl.BlockSpec((64, BLOCK), lambda i: (0, 0))
    return pl.pallas_call(
        raw_kernel,
        grid=(count // rows,),
        in_specs=[
            pl.BlockSpec((rows, WIDTH), lambda i: (i, 0)),
            piece,
            piece,
            piece,
            piece,
            pl.BlockSpec(memory_space=pl.ANY),
        ],
        out_specs=pl.BlockSpec((rows, BLOCK), lambda i: (i, 1)),
        out_shape=pltpu.HBM(result.shape, F32),
        scratch_shapes=[pltpu.VMEM((WIDTH, BLOCK), F32), pltpu.VMEM((WIDTH, WIDTH), BF16)],
        input_output_aliases={5: 0},
        compiler_params=pltpu.CompilerParams(vmem_limit_bytes=VMEM_LIMIT),
        cost_estimate=cost(count),
    )(raw, *pieces, result)


def per_device(slab, block_ids):
    core, _ = place()
    parts, raw = summed_over_rows(local_gram(slab), core, slab[:RAW])
    *leaving, rot_stay, diag = rounds_and_leaving(parts, slab, block_ids)
    leaving[0], raw = lax.optimization_barrier((leaving[0], raw))
    arrived = [passed_along(chunk) for chunk in leaving]
    extra = arrived[0][CHUNKS[0] :]
    new_slab = staying(slab, rot_stay)
    new_slab = rotated_raw(raw, with_three_others(extra[:64], 1), new_slab)
    for n, chunk in enumerate(arrived):
        start = (RAW + sum(CHUNKS[:n]), BLOCK)
        new_slab = lax.dynamic_update_slice(new_slab, chunk[: CHUNKS[n]], start)
    total_rows = slab.shape[0] * lax.axis_size("row")
    squares = jnp.concatenate([diag[0, :BLOCK], extra[64]])
    col_norms = jnp.sqrt(jnp.maximum(squares, 0.0) / total_rows)
    new_ids = jnp.stack([jnp.min(block_ids), extra[72, 0].astype(jnp.int32)])
    return (new_slab, col_norms, new_ids)


def solution(mesh):
    return jax.shard_map(
        per_device,
        mesh=mesh,
        in_specs=(P("row", "pair"), P("pair")),
        out_specs=(P("row", "pair"), P("pair"), P("pair")),
        check_vma=False,
    )
```

```python
import functools

import jax
import jax.numpy as jnp
from jax import lax
from jax.experimental import pallas as pl
from jax.experimental.pallas import tpu as pltpu
from jax.sharding import PartitionSpec as P

ROUNDS = 48
BLOCK = 128
WIDTH = 256
F32 = jnp.float32
BF16 = jnp.bfloat16
HIGHEST = lax.Precision.HIGHEST
VMEM_LIMIT = 32 * 1024 * 1024
ROWS = 4096
RAW = 640
CHUNKS = (1024, 1792, ROWS - RAW - 2816)
EXTRA = 40
STEP = 256
PACKED = 272
PARTS = 4


def product(a, b):
    return jnp.dot(a, b, preferred_element_type=F32)


def product_over_rows(a, b):
    return lax.dot_general(a, b, (((0,), (0,)), ((), ())), preferred_element_type=F32)


def gram_kernel(slab_ref, out_ref, x_ref, even, odd, sems):
    rows = ROWS // PARTS
    parts = [pl.ds(n * rows, rows) for n in range(PARTS)]
    copies = [
        pltpu.make_async_copy(slab_ref.at[part, :], x_ref.at[part, :], sems.at[n])
        for n, part in enumerate(parts)
    ]
    for copy in copies:
        copy.start()
    for n, part in enumerate(parts):
        copies[n].wait()
        x = x_ref[part, :]
        high = x.astype(BF16)
        rest = x - high.astype(F32)
        mid = rest.astype(BF16)
        low = (rest - mid.astype(F32)).astype(BF16)
        same = product_over_rows(high, high) + product_over_rows(mid, mid)
        cross = product_over_rows(high, mid) + product_over_rows(high, low)
        even[...] = same if n == 0 else even[...] + same
        odd[...] = cross if n == 0 else odd[...] + cross
    gram = even[...] + odd[...] + odd[...].T
    row = lax.broadcasted_iota(jnp.int32, (BLOCK, BLOCK), 0)
    col = lax.broadcasted_iota(jnp.int32, (BLOCK, BLOCK), 1)
    last = gram[128:256, 128:256]
    out_ref[0:128, :] = jnp.where(row <= col, gram[0:128, 0:128], last)
    out_ref[128:256, :] = gram[0:128, 128:256]
    diag = jnp.sum(jnp.where(row == col, last, 0.0), axis=0, keepdims=True)
    out_ref[256:272, :] = jnp.broadcast_to(diag, (16, BLOCK))


def local_gram(slab):
    return pl.pallas_call(
        gram_kernel,
        in_specs=[pl.BlockSpec(memory_space=pl.ANY)],
        out_specs=pl.BlockSpec(memory_space=pltpu.VMEM),
        out_shape=jax.ShapeDtypeStruct((PACKED, BLOCK), F32),
        scratch_shapes=[
            pltpu.VMEM((ROWS, WIDTH), F32),
            pltpu.VMEM((WIDTH, WIDTH), F32),
            pltpu.VMEM((WIDTH, WIDTH), F32),
            pltpu.SemaphoreType.DMA((PARTS,)),
        ],
        compiler_params=pltpu.CompilerParams(vmem_limit_bytes=VMEM_LIMIT),
    )(pltpu.with_memory_space_constraint(slab, pltpu.HBM))


def place():
    me = lax.axis_index("row")
    return me & 1, (me >> 1) & 3


def exchanged(array, mask):
    return lax.ppermute(array, "row", [(i, i ^ mask) for i in range(128)])


def passed_along(array):
    return lax.ppermute(array, "pair", [(0, 1), (1, 0)])


def with_three_others(mine, shift):
    return [mine] + [exchanged(mine, d << shift) for d in (1, 2, 3)]


def summed_over_four(mine, shift):
    parts = with_three_others(mine, shift)
    return (parts[0] + parts[2]) + (parts[1] + parts[3])


def summed_over_rows(part, core, raw):
    half = part.shape[0] // 2
    mine = lax.dynamic_slice_in_dim(part, core * half, half, 0)
    yours = lax.dynamic_slice_in_dim(part, (1 - core) * half, half, 0)
    total = summed_over_four(mine + exchanged(yours, 1), 5)
    raw, total = lax.optimization_barrier((raw, total))
    raw_arrived = passed_along(raw)
    total = summed_over_four(summed_over_four(total, 1), 3)
    return (total, exchanged(total, 1)), raw_arrived


def angles(g, d_top, d_bot):
    diff = d_bot - d_top
    sgn = jnp.where(diff >= 0, 1.0, -1.0)
    den = jnp.abs(diff) + jnp.sqrt(diff * diff + 4.0 * g * g)
    tang = jnp.where(den > 0, 2.0 * g * sgn / jnp.where(den > 0, den, 1.0), 0.0)
    cosv = 1.0 / jnp.sqrt(1.0 + tang * tang)
    return tang, cosv, tang * cosv

def rounds_kernel(
    ids_ref, mine_ref, other_ref, slab_ref, first_ref, leave_ref, stay_ref, diag_ref,
    packed, vt, vb, wt, wb, x_ref, sem,
):
    rounds = ROUNDS
    fetch = pltpu.make_async_copy(slab_ref.at[pl.ds(RAW, CHUNKS[0]), :], x_ref, sem)
    fetch.start()
    core, x = place()
    swap = (ids_ref[1] <= ids_ref[0]).astype(jnp.int32)
    for h, part in enumerate((mine_ref, other_ref)):
        start = pl.multiple_of((core ^ h) * (PACKED // 2), 8)
        packed[pl.ds(start, PACKED // 2), :] = part[...]
    half = 128
    lane = lax.broadcasted_iota(jnp.int32, (8, half), 1)
    first, last = lane == 0, lane == half - 1
    row = lax.broadcasted_iota(jnp.int32, (2 * half, half), 0)
    col = lax.broadcasted_iota(jnp.int32, (2 * half, half), 1)
    vt[...] = (row == col).astype(F32)
    vb[...] = (row == 255 - col).astype(F32)
    both, b = packed[0:128, :], packed[128:256, :]
    mirrored = both.T
    above, below = row[:half] < col[:half], row[:half] > col[:half]
    a = jnp.where(below, mirrored, both)
    c = jnp.where(below, both, jnp.where(above, mirrored, packed[256:257, :]))
    rev = (row[:half] == half - 1 - col[:half]).astype(F32)
    wt[0:128, :] = a
    wt[128:256, :] = b.T
    wb[0:128, :] = jnp.dot(b, rev, precision=HIGHEST, preferred_element_type=F32)
    wb[128:256, :] = jnp.dot(c, rev, precision=HIGHEST, preferred_element_type=F32)
    eye = row[:half] == col[:half]
    d_top = jnp.sum(jnp.where(eye, wt[0:128, :], 0.0), axis=0, keepdims=True)
    anti = row[:half] == half - 1 - col[:half]
    d_bot = jnp.sum(jnp.where(anti, wb[128:256, :], 0.0), axis=0, keepdims=True)
    g = (jnp.sum(jnp.where(eye, wb[0:128, :], 0.0), axis=0, keepdims=True))
    d_top, d_bot, g = (jnp.broadcast_to(v, (8, half)) for v in (d_top, d_bot, g))

    def shifted(top, bot):
        new_top = jnp.where(last, bot, pltpu.roll(top, half - 1, 1))
        new_bot = jnp.where(first, bot, pltpu.roll(jnp.where(first, top, bot), 1, 1))
        return new_top, new_bot

    def one_round(_, state):
        g, d_top, d_bot = state
        t, c, s = angles(g, d_top, d_bot)
        d_top, d_bot = shifted(d_top - t * g, d_bot + t * g)
        acc = [jnp.zeros((8, half), F32) for _ in range(4)]
        for k in range(32):
            sl = pl.ds(8 * k, 8)
            a, b = vt[sl, :], vb[sl, :]
            nvt, nvb = shifted(c * a - s * b, s * a + c * b)
            vt[sl, :] = nvt
            vb[sl, :] = nvb
            a, b = wt[sl, :], wb[sl, :]
            nwt, nwb = shifted(c * a - s * b, s * a + c * b)
            wt[sl, :] = nwt
            wb[sl, :] = nwb
            acc[k % 4] = acc[k % 4] + nvt * nwb
        g = jnp.sum((acc[0] + acc[1]) + (acc[2] + acc[3]), axis=0, keepdims=True)
        return jnp.broadcast_to(g, (8, half)), d_top, d_bot

    g, d_top, d_bot = lax.fori_loop(0, rounds, one_round, (g, d_top, d_bot))
    r = lax.broadcasted_iota(jnp.int32, (half, 2 * half), 0)
    j = lax.broadcasted_iota(jnp.int32, (half, 2 * half), 1)
    idx = jnp.where(swap > 0, jnp.where(j >= half, j - half, j + half), j)
    p_top = (r + rounds == idx).astype(F32)
    back = rounds - idx
    back = jnp.where(idx == 2 * half - 1, 0, jnp.where(back <= 0, back + 255, back))
    p_bot = ((r == back) & ((idx < rounds) | (idx >= rounds + half))).astype(F32)
    dot = functools.partial(jnp.dot, precision=HIGHEST, preferred_element_type=F32)
    rot = dot(vt[...], p_top) + dot(vb[...], p_bot)
    high = rot.astype(BF16)
    low = (rot - high.astype(F32)).astype(BF16)
    stay_ref[:, 0:128] = high[:, 0:128]
    stay_ref[:, 128:256] = low[:, 0:128]
    leave_ref[:, 0:128] = high[:, 128:256]
    leave_ref[:, 128:256] = low[:, 128:256]
    diag = dot(d_top, p_top) + dot(d_bot, p_bot)
    diag_ref[...] = diag
    wt[...] = rot[:, 128:256]
    piece = pl.ds(pl.multiple_of((2 * x + core) * 32, 32), 32)
    first_ref[CHUNKS[0] : CHUNKS[0] + 32, :] = wt[piece, :]
    label = jnp.full((8, half), jnp.maximum(ids_ref[0], ids_ref[1]).astype(F32))
    upper = lax.broadcasted_iota(jnp.int32, (8, half), 0) < 4
    first_ref[CHUNKS[0] + 32 : CHUNKS[0] + 40, :] = jnp.where(upper, diag[:, 128:256], label)
    fetch.wait()
    for start in range(0, CHUNKS[0], STEP):
        first_ref[start : start + STEP, :] = rotation(x_ref[start : start + STEP, :], leave_ref[...])


def rotation(x, rot):
    high = x.astype(BF16)
    low = (x - high.astype(F32)).astype(BF16)
    both = product(high, rot)
    return (both[:, 0:128] + both[:, 128:256]) + product(low, rot[:, 0:128])


def rounds_and_first_chunk(parts, slab, block_ids):
    in_vmem = pl.BlockSpec(memory_space=pltpu.VMEM)
    return pl.pallas_call(
        rounds_kernel,
        in_specs=[
            pl.BlockSpec(memory_space=pltpu.SMEM),
            in_vmem,
            in_vmem,
            pl.BlockSpec(memory_space=pl.ANY),
        ],
        out_specs=(in_vmem,) * 4,
        out_shape=(
            jax.ShapeDtypeStruct((CHUNKS[0] + EXTRA, BLOCK), F32),
            jax.ShapeDtypeStruct((WIDTH, WIDTH), BF16),
            jax.ShapeDtypeStruct((WIDTH, WIDTH), BF16),
            jax.ShapeDtypeStruct((8, WIDTH), F32),
        ),
        scratch_shapes=[pltpu.VMEM((PACKED, BLOCK), F32)]
        + [pltpu.VMEM((WIDTH, BLOCK), F32)] * 4
        + [
            pltpu.VMEM((CHUNKS[0], WIDTH), F32),
            pltpu.SemaphoreType.DMA,
        ],
        compiler_params=pltpu.CompilerParams(vmem_limit_bytes=VMEM_LIMIT),
        cost_estimate=pl.CostEstimate(flops=0, bytes_accessed=0, transcendentals=0),
    )(block_ids, *parts, pltpu.with_memory_space_constraint(slab, pltpu.HBM))


def cost(count):
    return pl.CostEstimate(
        flops=6 * count * WIDTH * BLOCK, bytes_accessed=6 * count * WIDTH, transcendentals=0
    )


def rotate_kernel(x_ref, rot_ref, out_ref):
    out_ref[...] = rotation(x_ref[...], rot_ref[...])


def leaving(slab, rot, first, count, rows=128):
    return pl.pallas_call(
        rotate_kernel,
        grid=(count // rows,),
        in_specs=[
            pl.BlockSpec((rows, WIDTH), lambda i: (i + first // rows, 0)),
            pl.BlockSpec((WIDTH, WIDTH), lambda i: (0, 0)),
        ],
        out_specs=pl.BlockSpec((rows, BLOCK), lambda i: (i, 0)),
        out_shape=jax.ShapeDtypeStruct((count, BLOCK), F32),
        compiler_params=pltpu.CompilerParams(vmem_limit_bytes=VMEM_LIMIT),
        cost_estimate=cost(count),
    )(pltpu.with_memory_space_constraint(slab, pltpu.HBM), rot)


def staying(slab, rot, rows=512):
    count = slab.shape[0]
    return pl.pallas_call(
        rotate_kernel,
        grid=(count // rows,),
        in_specs=[
            pl.BlockSpec((rows, WIDTH), lambda i: (i, 0)),
            pl.BlockSpec((WIDTH, WIDTH), lambda i: (0, 0)),
        ],
        out_specs=pl.BlockSpec((rows, BLOCK), lambda i: (i, 0)),
        out_shape=pltpu.HBM((count, WIDTH), F32),
        compiler_params=pltpu.CompilerParams(vmem_limit_bytes=VMEM_LIMIT),
        cost_estimate=cost(count),
    )(pltpu.with_memory_space_constraint(slab, pltpu.HBM), rot)


def raw_kernel(x_ref, p0_ref, p1_ref, p2_ref, p3_ref, _, out_ref, full, rot):
    @pl.when(pl.program_id(0) == 0)
    def _():
        for d, piece in enumerate((p0_ref, p1_ref, p2_ref, p3_ref)):
            for h in range(2):
                start = (2 * (place()[1] ^ d) + (place()[0] ^ h)) * 32
                full[pl.ds(pl.multiple_of(start, 32), 32), :] = piece[32 * h : 32 * h + 32, :]
        high = full[...].astype(BF16)
        rot[:, 0:128] = high
        rot[:, 128:256] = (full[...] - high.astype(F32)).astype(BF16)

    out_ref[...] = rotation(x_ref[...], rot[...])


def rotated_raw(raw, pieces, result, rows=128):
    count = raw.shape[0]
    piece = pl.BlockSpec((64, BLOCK), lambda i: (0, 0))
    return pl.pallas_call(
        raw_kernel,
        grid=(count // rows,),
        in_specs=[
            pl.BlockSpec((rows, WIDTH), lambda i: (i, 0)),
            piece,
            piece,
            piece,
            piece,
            pl.BlockSpec(memory_space=pl.ANY),
        ],
        out_specs=pl.BlockSpec((rows, BLOCK), lambda i: (i, 1)),
        out_shape=pltpu.HBM(result.shape, F32),
        scratch_shapes=[pltpu.VMEM((WIDTH, BLOCK), F32), pltpu.VMEM((WIDTH, WIDTH), BF16)],
        input_output_aliases={5: 0},
        compiler_params=pltpu.CompilerParams(vmem_limit_bytes=VMEM_LIMIT),
        cost_estimate=cost(count),
    )(raw, *pieces, result)


def per_device(slab, block_ids):
    core, _ = place()
    parts, raw = summed_over_rows(local_gram(slab), core, slab[:RAW])
    first, rot_leave, rot_stay, diag = rounds_and_first_chunk(parts, slab, block_ids)
    first, raw = lax.optimization_barrier((first, raw))
    arrived = [passed_along(first)]
    extra = arrived[0][CHUNKS[0] :]
    starts = [RAW + sum(CHUNKS[:n]) for n in range(len(CHUNKS))]
    for start, count in zip(starts[1:], CHUNKS[1:]):
        arrived.append(passed_along(leaving(slab, rot_leave, start, count)))
    new_slab = staying(slab, rot_stay)
    both = jnp.concatenate([extra[:32], exchanged(extra[:32], 1)])
    new_slab = rotated_raw(raw, with_three_others(both, 1), new_slab)
    for start, count, chunk in zip(starts, CHUNKS, arrived):
        new_slab = lax.dynamic_update_slice(new_slab, chunk[:count], (start, BLOCK))
    total_rows = slab.shape[0] * lax.axis_size("row")
    squares = jnp.concatenate([diag[0, :BLOCK], extra[32]])
    col_norms = jnp.sqrt(jnp.maximum(squares, 0.0) / total_rows)
    new_ids = jnp.stack([jnp.min(block_ids), extra[36, 0].astype(jnp.int32)])
    return (new_slab, col_norms, new_ids)


def solution(mesh):
    return jax.shard_map(
        per_device,
        mesh=mesh,
        in_specs=(P("row", "pair"), P("pair")),
        out_specs=(P("row", "pair"), P("pair"), P("pair")),
        check_vma=False,
    )
```

```python
import functools

import jax
import jax.numpy as jnp
import numpy as np
from jax import lax
from jax.experimental import pallas as pl
from jax.experimental.pallas import tpu as pltpu
from jax.sharding import PartitionSpec as P

ROUNDS = 48
BLOCK = 128
WIDTH = 256
F32 = jnp.float32
BF16 = jnp.bfloat16
HIGHEST = lax.Precision.HIGHEST
VMEM_LIMIT = 32 * 1024 * 1024
ROWS = 4096
RAW = 512
CHUNKS = (1536 - RAW, 1792, 768)
EXTRA = 40
STEP = CHUNKS[0] // 4
PACKED = 272
PARTS = 4


def product(a, b):
    return jnp.dot(a, b, preferred_element_type=F32)


def product_over_rows(a, b):
    return lax.dot_general(a, b, (((0,), (0,)), ((), ())), preferred_element_type=F32)


def gram_kernel(slab_ref, out_ref, x_ref, even, odd, sems):
    rows = ROWS // PARTS
    parts = [pl.ds(n * rows, rows) for n in range(PARTS)]
    copies = [
        pltpu.make_async_copy(slab_ref.at[part, :], x_ref.at[part, :], sems.at[n])
        for n, part in enumerate(parts)
    ]
    for copy in copies:
        copy.start()
    for n, part in enumerate(parts):
        copies[n].wait()
        x = x_ref[part, :]
        high = x.astype(BF16)
        rest = x - high.astype(F32)
        mid = rest.astype(BF16)
        low = (rest - mid.astype(F32)).astype(BF16)
        same = product_over_rows(high, high) + product_over_rows(mid, mid)
        cross = product_over_rows(high, mid) + product_over_rows(high, low)
        even[...] = same if n == 0 else even[...] + same
        odd[...] = cross if n == 0 else odd[...] + cross
    gram = even[...] + odd[...] + odd[...].T
    row = lax.broadcasted_iota(jnp.int32, (BLOCK, BLOCK), 0)
    col = lax.broadcasted_iota(jnp.int32, (BLOCK, BLOCK), 1)
    last = gram[128:256, 128:256]
    out_ref[0:128, :] = jnp.where(row <= col, gram[0:128, 0:128], last)
    out_ref[128:256, :] = gram[0:128, 128:256]
    diag = jnp.sum(jnp.where(row == col, last, 0.0), axis=0, keepdims=True)
    out_ref[256:272, :] = jnp.broadcast_to(diag, (16, BLOCK))


def local_gram(slab):
    return pl.pallas_call(
        gram_kernel,
        in_specs=[pl.BlockSpec(memory_space=pl.ANY)],
        out_specs=pl.BlockSpec(memory_space=pltpu.VMEM),
        out_shape=jax.ShapeDtypeStruct((PACKED, BLOCK), F32),
        scratch_shapes=[
            pltpu.VMEM((ROWS, WIDTH), F32),
            pltpu.VMEM((WIDTH, WIDTH), F32),
            pltpu.VMEM((WIDTH, WIDTH), F32),
            pltpu.SemaphoreType.DMA((PARTS,)),
        ],
        compiler_params=pltpu.CompilerParams(vmem_limit_bytes=VMEM_LIMIT),
    )(pltpu.with_memory_space_constraint(slab, pltpu.HBM))


def place():
    me = lax.axis_index("row")
    return me & 1, (me >> 1) & 3


def exchanged(array, mask):
    return lax.ppermute(array, "row", [(i, i ^ mask) for i in range(128)])


def passed_along(array):
    return lax.ppermute(array, "pair", [(0, 1), (1, 0)])


def with_three_others(mine, shift):
    return [mine] + [exchanged(mine, d << shift) for d in (1, 2, 3)]


def summed_over_four(mine, shift):
    parts = with_three_others(mine, shift)
    return (parts[0] + parts[2]) + (parts[1] + parts[3])


def summed_over_rows(part, core, raw):
    half = part.shape[0] // 2
    mine = lax.dynamic_slice_in_dim(part, core * half, half, 0)
    yours = lax.dynamic_slice_in_dim(part, (1 - core) * half, half, 0)
    total = summed_over_four(mine + exchanged(yours, 1), 5)
    raw, total = lax.optimization_barrier((raw, total))
    raw_arrived = passed_along(raw)
    total = summed_over_four(summed_over_four(total, 1), 3)
    return (total, exchanged(total, 1)), raw_arrived


def meetings(step):
    ring = WIDTH - 1
    return [(step, ring)] + [((step + k) % ring, (step - k) % ring) for k in range(1, BLOCK)]


def round_tables():
    top, bottom = np.arange(BLOCK), WIDTH - 1 - np.arange(BLOCK)
    table = np.zeros((ROUNDS, 8, BLOCK), np.int32)
    table[:, 0] = np.arange(BLOCK)
    for step in range(ROUNDS):
        first = {i for i, _ in meetings(step)}
        table[step, 2] = [t in first for t in top]
        if step == ROUNDS - 1:
            break
        now, later = np.zeros(WIDTH, int), np.zeros(WIDTH, int)
        for pairs, partner in ((meetings(step), now), (meetings(step + 1), later)):
            for i, j in pairs:
                partner[i], partner[j] = j, i
        side = np.full(WIDTH, -1)
        for member in range(WIDTH):
            while side[member] < 0:
                side[member], side[now[member]] = 0, 1
                member = later[now[member]]
        swap = side[top] == 1
        table[step, 1] = swap
        top, bottom = np.where(swap, bottom, top), np.where(swap, top, bottom)
        lane = np.zeros(WIDTH, int)
        lane[bottom] = np.arange(BLOCK)
        table[step, 0] = lane[later[top]]
        bottom = later[top]
    last = np.concatenate([top, bottom]).astype(np.int32)
    return table, np.repeat(last[:, None], BLOCK, axis=1)


def angles(g, d_top, d_bot, top_first):
    diff = d_bot - d_top
    double = jnp.where((diff > 0) | ((diff == 0) & top_first), 2.0 * g, -2.0 * g)
    den = jnp.abs(diff) + jnp.sqrt(diff * diff + 4.0 * g * g)
    tang = jnp.where(den > 0, double / jnp.where(den > 0, den, 1.0), 0.0)
    cosv = lax.rsqrt(1.0 + tang * tang)
    return tang, cosv, tang * cosv


def rounds_kernel(
    ids_ref, table_ref, last_ref, mine_ref, other_ref, slab_ref, first_ref, leave_ref, stay_ref, diag_ref,
    packed, vt, vb, wt, wb, start_ref, x_ref, sem,
):
    fetch = pltpu.make_async_copy(slab_ref.at[pl.ds(RAW, CHUNKS[0]), :], x_ref, sem)
    fetch.start()
    core, x = place()
    swap_blocks = (ids_ref[1] <= ids_ref[0]).astype(jnp.int32)
    for h, part in enumerate((mine_ref, other_ref)):
        start = pl.multiple_of((core ^ h) * (PACKED // 2), 8)
        packed[pl.ds(start, PACKED // 2), :] = part[...]
    half = BLOCK
    row = lax.broadcasted_iota(jnp.int32, (2 * half, half), 0)
    col = lax.broadcasted_iota(jnp.int32, (2 * half, half), 1)
    vt[...] = (row == col).astype(F32)
    vb[...] = (row == 255 - col).astype(F32)
    both, b = packed[0:128, :], packed[128:256, :]
    mirrored = both.T
    above, below = row[:half] < col[:half], row[:half] > col[:half]
    a = jnp.where(below, mirrored, both)
    c = jnp.where(below, both, jnp.where(above, mirrored, packed[256:257, :]))
    rev = (row[:half] == half - 1 - col[:half]).astype(F32)
    wt[0:128, :] = a
    wt[128:256, :] = b.T
    wb[0:128, :] = jnp.dot(b, rev, precision=HIGHEST, preferred_element_type=F32)
    wb[128:256, :] = jnp.dot(c, rev, precision=HIGHEST, preferred_element_type=F32)
    eye = row[:half] == col[:half]
    d_top = jnp.sum(jnp.where(eye, wt[0:128, :], 0.0), axis=0, keepdims=True)
    anti = row[:half] == half - 1 - col[:half]
    d_bot = jnp.sum(jnp.where(anti, wb[128:256, :], 0.0), axis=0, keepdims=True)
    g = (jnp.sum(jnp.where(eye, wb[0:128, :], 0.0), axis=0, keepdims=True))
    for n, v in enumerate((g, d_top, d_bot)):
        start_ref[n] = jnp.broadcast_to(v, (8, half))

    def one_round(step, state):
        g, d_top, d_bot = state
        source, swap, top_first = (
            jnp.broadcast_to(table_ref[step, n : n + 1, :], (8, half)) for n in range(3)
        )
        swap = swap > 0

        def moved(bottom):
            return jnp.take_along_axis(bottom, source, axis=1, mode="promise_in_bounds")

        t, c, s = angles(g, d_top, d_bot, top_first > 0)
        a, b = d_top - t * g, d_bot + t * g
        d_top, d_bot = jnp.where(swap, b, a), moved(jnp.where(swap, a, b))
        top_a, top_b = jnp.where(swap, s, c), jnp.where(swap, c, -s)
        bot_a, bot_b = jnp.where(swap, c, s), jnp.where(swap, -s, c)
        acc = [jnp.zeros((8, half), F32) for _ in range(4)]
        for k in range(32):
            sl = pl.ds(8 * k, 8)
            a, b = vt[sl, :], vb[sl, :]
            new_vt = top_a * a + top_b * b
            vt[sl, :] = new_vt
            vb[sl, :] = moved(bot_a * a + bot_b * b)
            a, b = wt[sl, :], wb[sl, :]
            wt[sl, :] = top_a * a + top_b * b
            new_wb = moved(bot_a * a + bot_b * b)
            wb[sl, :] = new_wb
            acc[k % 4] = acc[k % 4] + new_vt * new_wb
        g = jnp.sum((acc[0] + acc[1]) + (acc[2] + acc[3]), axis=0, keepdims=True)
        return jnp.broadcast_to(g, (8, half)), d_top, d_bot

    g, d_top, d_bot = lax.fori_loop(0, ROUNDS, one_round, tuple(start_ref[n] for n in range(3)))
    dot = functools.partial(jnp.dot, precision=HIGHEST, preferred_element_type=F32)
    lane = lax.broadcasted_iota(jnp.int32, (half, half), 1)
    halves, diags = [], []
    for n in range(2):
        column = lane + half * (n ^ swap_blocks)
        p_top = (last_ref[0:half, :] == column).astype(F32)
        p_bot = (last_ref[half : 2 * half, :] == column).astype(F32)
        halves.append(dot(vt[...], p_top) + dot(vb[...], p_bot))
        diags.append(dot(d_top, p_top) + dot(d_bot, p_bot))
    rot = jnp.concatenate(halves, axis=1)
    high = rot.astype(BF16)
    low = (rot - high.astype(F32)).astype(BF16)
    stay_ref[:, 0:128] = high[:, 0:128]
    stay_ref[:, 128:256] = low[:, 0:128]
    leave_ref[:, 0:128] = high[:, 128:256]
    leave_ref[:, 128:256] = low[:, 128:256]
    diag = jnp.concatenate(diags, axis=1)
    diag_ref[...] = diag
    wt[...] = rot[:, 128:256]
    piece = pl.ds(pl.multiple_of((2 * x + core) * 32, 32), 32)
    first_ref[CHUNKS[0] : CHUNKS[0] + 32, :] = wt[piece, :]
    label = jnp.full((8, half), jnp.maximum(ids_ref[0], ids_ref[1]).astype(F32))
    upper = lax.broadcasted_iota(jnp.int32, (8, half), 0) < 4
    first_ref[CHUNKS[0] + 32 : CHUNKS[0] + 40, :] = jnp.where(upper, diag[:, 128:256], label)
    fetch.wait()
    for start in range(0, CHUNKS[0], STEP):
        first_ref[start : start + STEP, :] = rotation(x_ref[start : start + STEP, :], leave_ref[...])


def rotation(x, rot):
    high = x.astype(BF16)
    low = (x - high.astype(F32)).astype(BF16)
    both = product(high, rot)
    return (both[:, 0:128] + both[:, 128:256]) + product(low, rot[:, 0:128])


def rounds_and_first_chunk(parts, slab, block_ids):
    in_vmem = pl.BlockSpec(memory_space=pltpu.VMEM)
    return pl.pallas_call(
        rounds_kernel,
        in_specs=[
            pl.BlockSpec(memory_space=pltpu.SMEM),
            in_vmem,
            in_vmem,
            in_vmem,
            in_vmem,
            pl.BlockSpec(memory_space=pl.ANY),
        ],
        out_specs=(in_vmem,) * 4,
        out_shape=(
            jax.ShapeDtypeStruct((CHUNKS[0] + EXTRA, BLOCK), F32),
            jax.ShapeDtypeStruct((WIDTH, WIDTH), BF16),
            jax.ShapeDtypeStruct((WIDTH, WIDTH), BF16),
            jax.ShapeDtypeStruct((8, WIDTH), F32),
        ),
        scratch_shapes=[pltpu.VMEM((PACKED, BLOCK), F32)]
        + [pltpu.VMEM((WIDTH, BLOCK), F32)] * 4
        + [
            pltpu.VMEM((3, 8, BLOCK), F32),
            pltpu.VMEM((CHUNKS[0], WIDTH), F32),
            pltpu.SemaphoreType.DMA,
        ],
        compiler_params=pltpu.CompilerParams(vmem_limit_bytes=VMEM_LIMIT),
        cost_estimate=pl.CostEstimate(flops=0, bytes_accessed=0, transcendentals=0),
    )(block_ids, *(jnp.asarray(t) for t in round_tables()), *parts, pltpu.with_memory_space_constraint(slab, pltpu.HBM))


def cost(count):
    return pl.CostEstimate(
        flops=6 * count * WIDTH * BLOCK, bytes_accessed=6 * count * WIDTH, transcendentals=0
    )


def rotate_kernel(x_ref, rot_ref, out_ref):
    out_ref[...] = rotation(x_ref[...], rot_ref[...])


def leaving(slab, rot, first, count, rows=256):
    return pl.pallas_call(
        rotate_kernel,
        grid=(count // rows,),
        in_specs=[
            pl.BlockSpec((rows, WIDTH), lambda i: (i + first // rows, 0)),
            pl.BlockSpec((WIDTH, WIDTH), lambda i: (0, 0)),
        ],
        out_specs=pl.BlockSpec((rows, BLOCK), lambda i: (i, 0)),
        out_shape=jax.ShapeDtypeStruct((count, BLOCK), F32),
        compiler_params=pltpu.CompilerParams(vmem_limit_bytes=VMEM_LIMIT),
        cost_estimate=cost(count),
    )(pltpu.with_memory_space_constraint(slab, pltpu.HBM), rot)


def staying(slab, rot, rows=512):
    count = slab.shape[0]
    return pl.pallas_call(
        rotate_kernel,
        grid=(count // rows,),
        in_specs=[
            pl.BlockSpec((rows, WIDTH), lambda i: (i, 0)),
            pl.BlockSpec((WIDTH, WIDTH), lambda i: (0, 0)),
        ],
        out_specs=pl.BlockSpec((rows, BLOCK), lambda i: (i, 0)),
        out_shape=pltpu.HBM((count, WIDTH), F32),
        compiler_params=pltpu.CompilerParams(vmem_limit_bytes=VMEM_LIMIT),
        cost_estimate=cost(count),
    )(pltpu.with_memory_space_constraint(slab, pltpu.HBM), rot)


def raw_kernel(x_ref, p0_ref, p1_ref, p2_ref, p3_ref, _, out_ref, full, rot):
    @pl.when(pl.program_id(0) == 0)
    def _():
        for d, piece in enumerate((p0_ref, p1_ref, p2_ref, p3_ref)):
            for h in range(2):
                start = (2 * (place()[1] ^ d) + (place()[0] ^ h)) * 32
                full[pl.ds(pl.multiple_of(start, 32), 32), :] = piece[32 * h : 32 * h + 32, :]
        high = full[...].astype(BF16)
        rot[:, 0:128] = high
        rot[:, 128:256] = (full[...] - high.astype(F32)).astype(BF16)

    out_ref[...] = rotation(x_ref[...], rot[...])


def rotated_raw(raw, pieces, result, rows=RAW // 4):
    count = raw.shape[0]
    piece = pl.BlockSpec((64, BLOCK), lambda i: (0, 0))
    return pl.pallas_call(
        raw_kernel,
        grid=(count // rows,),
        in_specs=[
            pl.BlockSpec((rows, WIDTH), lambda i: (i, 0)),
            piece,
            piece,
            piece,
            piece,
            pl.BlockSpec(memory_space=pl.ANY),
        ],
        out_specs=pl.BlockSpec((rows, BLOCK), lambda i: (i, 1)),
        out_shape=pltpu.HBM(result.shape, F32),
        scratch_shapes=[pltpu.VMEM((WIDTH, BLOCK), F32), pltpu.VMEM((WIDTH, WIDTH), BF16)],
        input_output_aliases={5: 0},
        compiler_params=pltpu.CompilerParams(vmem_limit_bytes=VMEM_LIMIT),
        cost_estimate=cost(count),
    )(raw, *pieces, result)


def per_device(slab, block_ids):
    core, _ = place()
    parts, raw = summed_over_rows(local_gram(slab), core, slab[:RAW])
    first, rot_leave, rot_stay, diag = rounds_and_first_chunk(parts, slab, block_ids)
    first, raw = lax.optimization_barrier((first, raw))
    arrived = [passed_along(first)]
    extra = arrived[0][CHUNKS[0] :]
    starts = [RAW + sum(CHUNKS[:n]) for n in range(len(CHUNKS))]
    for start, count in zip(starts[1:], CHUNKS[1:]):
        arrived.append(passed_along(leaving(slab, rot_leave, start, count)))
    new_slab = staying(slab, rot_stay)
    both = jnp.concatenate([extra[:32], exchanged(extra[:32], 1)])
    new_slab = rotated_raw(raw, with_three_others(both, 1), new_slab)
    for start, count, chunk in zip(starts, CHUNKS, arrived):
        new_slab = lax.dynamic_update_slice(new_slab, chunk[:count], (start, BLOCK))
    total_rows = slab.shape[0] * lax.axis_size("row")
    squares = jnp.concatenate([diag[0, :BLOCK], extra[32]])
    col_norms = jnp.sqrt(jnp.maximum(squares, 0.0) / total_rows)
    new_ids = jnp.stack([jnp.min(block_ids), extra[36, 0].astype(jnp.int32)])
    return (new_slab, col_norms, new_ids)


def solution(mesh):
    return jax.shard_map(
        per_device,
        mesh=mesh,
        in_specs=(P("row", "pair"), P("pair")),
        out_specs=(P("row", "pair"), P("pair"), P("pair")),
        check_vma=False,
    )
```

```python
import functools

import jax
import jax.numpy as jnp
import numpy as np
from jax import lax
from jax.experimental import pallas as pl
from jax.experimental.pallas import tpu as pltpu
from jax.sharding import PartitionSpec as P

ROUNDS = 48
BLOCK = 128
WIDTH = 256
F32 = jnp.float32
BF16 = jnp.bfloat16
HIGHEST = lax.Precision.HIGHEST
VMEM_LIMIT = 32 * 1024 * 1024
ROWS = 4096
RAW = 512
CHUNKS = (1536 - RAW, 2304, 256)
EXTRA = 16
STEP = CHUNKS[0] // 4
PACKED = 272
PARTS = 4


def product(a, b):
    return jnp.dot(a, b, preferred_element_type=F32)


def product_over_rows(a, b):
    return lax.dot_general(a, b, (((0,), (0,)), ((), ())), preferred_element_type=F32)


def gram_kernel(slab_ref, out_ref, x_ref, even, odd, sems):
    rows = ROWS // PARTS
    parts = [pl.ds(n * rows, rows) for n in range(PARTS)]
    copies = [
        pltpu.make_async_copy(slab_ref.at[part, :], x_ref.at[part, :], sems.at[n])
        for n, part in enumerate(parts)
    ]
    for copy in copies:
        copy.start()
    for n, part in enumerate(parts):
        copies[n].wait()
        x = x_ref[part, :]
        high = x.astype(BF16)
        rest = x - high.astype(F32)
        mid = rest.astype(BF16)
        low = (rest - mid.astype(F32)).astype(BF16)
        same = product_over_rows(high, high) + product_over_rows(mid, mid)
        cross = product_over_rows(high, mid) + product_over_rows(high, low)
        even[...] = same if n == 0 else even[...] + same
        odd[...] = cross if n == 0 else odd[...] + cross
    gram = even[...] + odd[...] + odd[...].T
    row = lax.broadcasted_iota(jnp.int32, (BLOCK, BLOCK), 0)
    col = lax.broadcasted_iota(jnp.int32, (BLOCK, BLOCK), 1)
    last = gram[128:256, 128:256]
    out_ref[0:128, :] = jnp.where(row <= col, gram[0:128, 0:128], last)
    out_ref[128:256, :] = gram[0:128, 128:256]
    diag = jnp.sum(jnp.where(row == col, last, 0.0), axis=0, keepdims=True)
    out_ref[256:272, :] = jnp.broadcast_to(diag, (16, BLOCK))


def local_gram(slab):
    return pl.pallas_call(
        gram_kernel,
        in_specs=[pl.BlockSpec(memory_space=pl.ANY)],
        out_specs=pl.BlockSpec(memory_space=pltpu.VMEM),
        out_shape=jax.ShapeDtypeStruct((PACKED, BLOCK), F32),
        scratch_shapes=[
            pltpu.VMEM((ROWS, WIDTH), F32),
            pltpu.VMEM((WIDTH, WIDTH), F32),
            pltpu.VMEM((WIDTH, WIDTH), F32),
            pltpu.SemaphoreType.DMA((PARTS,)),
        ],
        compiler_params=pltpu.CompilerParams(vmem_limit_bytes=VMEM_LIMIT),
    )(pltpu.with_memory_space_constraint(slab, pltpu.HBM))


def place():
    me = lax.axis_index("row")
    return me & 1, (me >> 1) & 3, (me >> 3) & 3


def exchanged(array, mask):
    return lax.ppermute(array, "row", [(i, i ^ mask) for i in range(128)])


def passed_along(array):
    return lax.ppermute(array, "pair", [(0, 1), (1, 0)])


def with_three_others(mine, shift):
    return [mine] + [exchanged(mine, d << shift) for d in (1, 2, 3)]


def summed_over_four(mine, shift):
    parts = with_three_others(mine, shift)
    return (parts[0] + parts[2]) + (parts[1] + parts[3])


def summed_over_rows(part, core, raw):
    half = part.shape[0] // 2
    mine = lax.dynamic_slice_in_dim(part, core * half, half, 0)
    yours = lax.dynamic_slice_in_dim(part, (1 - core) * half, half, 0)
    total = summed_over_four(mine + exchanged(yours, 1), 5)
    raw, total = lax.optimization_barrier((raw, total))
    raw = passed_along(raw)
    total = summed_over_four(total, 1)
    total = summed_over_four(total, 3)
    return (total, exchanged(total, 1)), raw


def meetings(step):
    ring = WIDTH - 1
    return [(step, ring)] + [((step + k) % ring, (step - k) % ring) for k in range(1, BLOCK)]


def round_tables():
    top, bottom = np.arange(BLOCK), WIDTH - 1 - np.arange(BLOCK)
    table = np.zeros((ROUNDS, 8, BLOCK), np.int32)
    table[:, 0] = np.arange(BLOCK)
    for step in range(ROUNDS):
        first = {i for i, _ in meetings(step)}
        table[step, 2] = [t in first for t in top]
        if step == ROUNDS - 1:
            break
        now, later = np.zeros(WIDTH, int), np.zeros(WIDTH, int)
        for pairs, partner in ((meetings(step), now), (meetings(step + 1), later)):
            for i, j in pairs:
                partner[i], partner[j] = j, i
        side = np.full(WIDTH, -1)
        for member in range(WIDTH):
            while side[member] < 0:
                side[member], side[now[member]] = 0, 1
                member = later[now[member]]
        swap = side[top] == 1
        table[step, 1] = swap
        top, bottom = np.where(swap, bottom, top), np.where(swap, top, bottom)
        lane = np.zeros(WIDTH, int)
        lane[bottom] = np.arange(BLOCK)
        table[step, 0] = lane[later[top]]
        bottom = later[top]
    last = np.concatenate([top, bottom]).astype(np.int32)
    return table, np.repeat(last[:, None], BLOCK, axis=1)


def angles(g, d_top, d_bot, top_first):
    diff = d_bot - d_top
    double = jnp.where((diff > 0) | ((diff == 0) & top_first), 2.0 * g, -2.0 * g)
    den = jnp.abs(diff) + jnp.sqrt(diff * diff + 4.0 * g * g)
    tang = jnp.where(den > 0, double / jnp.where(den > 0, den, 1.0), 0.0)
    cosv = lax.rsqrt(1.0 + tang * tang)
    return tang, cosv, tang * cosv


def rounds_kernel(
    ids_ref, table_ref, last_ref, mine_ref, other_ref, slab_ref, first_ref, leave_ref, stay_ref, diag_ref,
    packed, vt, vb, wt, wb, start_ref, x_ref, sem,
):
    fetch = pltpu.make_async_copy(slab_ref.at[pl.ds(RAW, CHUNKS[0]), :], x_ref, sem)
    fetch.start()
    core, x, y = place()
    swap_blocks = (ids_ref[1] <= ids_ref[0]).astype(jnp.int32)
    for h, part in enumerate((mine_ref, other_ref)):
        start = pl.multiple_of((core ^ h) * (PACKED // 2), 8)
        packed[pl.ds(start, PACKED // 2), :] = part[...]
    half = BLOCK
    row = lax.broadcasted_iota(jnp.int32, (2 * half, half), 0)
    col = lax.broadcasted_iota(jnp.int32, (2 * half, half), 1)
    vt[...] = (row == col).astype(F32)
    vb[...] = (row == 255 - col).astype(F32)
    both, b = packed[0:128, :], packed[128:256, :]
    mirrored = both.T
    above, below = row[:half] < col[:half], row[:half] > col[:half]
    a = jnp.where(below, mirrored, both)
    c = jnp.where(below, both, jnp.where(above, mirrored, packed[256:257, :]))
    rev = (row[:half] == half - 1 - col[:half]).astype(F32)
    wt[0:128, :] = a
    wt[128:256, :] = b.T
    wb[0:128, :] = jnp.dot(b, rev, precision=HIGHEST, preferred_element_type=F32)
    wb[128:256, :] = jnp.dot(c, rev, precision=HIGHEST, preferred_element_type=F32)
    eye = row[:half] == col[:half]
    d_top = jnp.sum(jnp.where(eye, wt[0:128, :], 0.0), axis=0, keepdims=True)
    anti = row[:half] == half - 1 - col[:half]
    d_bot = jnp.sum(jnp.where(anti, wb[128:256, :], 0.0), axis=0, keepdims=True)
    g = (jnp.sum(jnp.where(eye, wb[0:128, :], 0.0), axis=0, keepdims=True))
    for n, v in enumerate((g, d_top, d_bot)):
        start_ref[n] = jnp.broadcast_to(v, (8, half))

    def one_round(step, state):
        g, d_top, d_bot = state
        source, swap, top_first = (
            jnp.broadcast_to(table_ref[step, n : n + 1, :], (8, half)) for n in range(3)
        )
        swap = swap > 0

        def moved(bottom):
            return jnp.take_along_axis(bottom, source, axis=1, mode="promise_in_bounds")

        t, c, s = angles(g, d_top, d_bot, top_first > 0)
        a, b = d_top - t * g, d_bot + t * g
        d_top, d_bot = jnp.where(swap, b, a), moved(jnp.where(swap, a, b))
        top_a, top_b = jnp.where(swap, s, c), jnp.where(swap, c, -s)
        bot_a, bot_b = jnp.where(swap, c, s), jnp.where(swap, -s, c)
        acc = [jnp.zeros((8, half), F32) for _ in range(4)]
        for k in range(32):
            sl = pl.ds(8 * k, 8)
            a, b = vt[sl, :], vb[sl, :]
            new_vt = top_a * a + top_b * b
            vt[sl, :] = new_vt
            vb[sl, :] = moved(bot_a * a + bot_b * b)
            a, b = wt[sl, :], wb[sl, :]
            wt[sl, :] = top_a * a + top_b * b
            new_wb = moved(bot_a * a + bot_b * b)
            wb[sl, :] = new_wb
            acc[k % 4] = acc[k % 4] + new_vt * new_wb
        g = jnp.sum((acc[0] + acc[1]) + (acc[2] + acc[3]), axis=0, keepdims=True)
        return jnp.broadcast_to(g, (8, half)), d_top, d_bot

    g, d_top, d_bot = lax.fori_loop(0, ROUNDS, one_round, tuple(start_ref[n] for n in range(3)))
    dot = functools.partial(jnp.dot, precision=HIGHEST, preferred_element_type=F32)
    lane = lax.broadcasted_iota(jnp.int32, (half, half), 1)
    halves, diags = [], []
    for n in range(2):
        column = lane + half * (n ^ swap_blocks)
        p_top = (last_ref[0:half, :] == column).astype(F32)
        p_bot = (last_ref[half : 2 * half, :] == column).astype(F32)
        halves.append(dot(vt[...], p_top) + dot(vb[...], p_bot))
        diags.append(dot(d_top, p_top) + dot(d_bot, p_bot))
    rot = jnp.concatenate(halves, axis=1)
    high = rot.astype(BF16)
    low = (rot - high.astype(F32)).astype(BF16)
    stay_ref[:, 0:128] = high[:, 0:128]
    stay_ref[:, 128:256] = low[:, 0:128]
    leave_ref[:, 0:128] = high[:, 128:256]
    leave_ref[:, 128:256] = low[:, 128:256]
    diag = jnp.concatenate(diags, axis=1)
    diag_ref[...] = diag
    wt[...] = rot[:, 128:256]
    piece = pl.ds(pl.multiple_of(((4 * y + x) * 2 + core) * 8, 8), 8)
    first_ref[CHUNKS[0] : CHUNKS[0] + 8, :] = wt[piece, :]
    label = jnp.full((8, half), jnp.maximum(ids_ref[0], ids_ref[1]).astype(F32))
    upper = lax.broadcasted_iota(jnp.int32, (8, half), 0) < 4
    first_ref[CHUNKS[0] + 8 : CHUNKS[0] + 16, :] = jnp.where(upper, diag[:, 128:256], label)
    fetch.wait()
    for start in range(0, CHUNKS[0], STEP):
        first_ref[start : start + STEP, :] = rotation(x_ref[start : start + STEP, :], leave_ref[...])


def rotation(x, rot):
    high = x.astype(BF16)
    low = (x - high.astype(F32)).astype(BF16)
    both = product(high, rot)
    return (both[:, 0:128] + both[:, 128:256]) + product(low, rot[:, 0:128])


def rounds_and_first_chunk(parts, slab, block_ids):
    in_vmem = pl.BlockSpec(memory_space=pltpu.VMEM)
    return pl.pallas_call(
        rounds_kernel,
        in_specs=[
            pl.BlockSpec(memory_space=pltpu.SMEM),
            in_vmem,
            in_vmem,
            in_vmem,
            in_vmem,
            pl.BlockSpec(memory_space=pl.ANY),
        ],
        out_specs=(in_vmem,) * 4,
        out_shape=(
            jax.ShapeDtypeStruct((CHUNKS[0] + EXTRA, BLOCK), F32),
            jax.ShapeDtypeStruct((WIDTH, WIDTH), BF16),
            jax.ShapeDtypeStruct((WIDTH, WIDTH), BF16),
            jax.ShapeDtypeStruct((8, WIDTH), F32),
        ),
        scratch_shapes=[pltpu.VMEM((PACKED, BLOCK), F32)]
        + [pltpu.VMEM((WIDTH, BLOCK), F32)] * 4
        + [
            pltpu.VMEM((3, 8, BLOCK), F32),
            pltpu.VMEM((CHUNKS[0], WIDTH), F32),
            pltpu.SemaphoreType.DMA,
        ],
        compiler_params=pltpu.CompilerParams(vmem_limit_bytes=VMEM_LIMIT),
        cost_estimate=pl.CostEstimate(flops=0, bytes_accessed=0, transcendentals=0),
    )(block_ids, *(jnp.asarray(t) for t in round_tables()), *parts, pltpu.with_memory_space_constraint(slab, pltpu.HBM))


def cost(count):
    return pl.CostEstimate(
        flops=6 * count * WIDTH * BLOCK, bytes_accessed=6 * count * WIDTH, transcendentals=0
    )


def rotate_kernel(x_ref, rot_ref, out_ref):
    out_ref[...] = rotation(x_ref[...], rot_ref[...])


def leaving(slab, rot, first, count, rows=256):
    return pl.pallas_call(
        rotate_kernel,
        grid=(count // rows,),
        in_specs=[
            pl.BlockSpec((rows, WIDTH), lambda i: (i + first // rows, 0)),
            pl.BlockSpec((WIDTH, WIDTH), lambda i: (0, 0)),
        ],
        out_specs=pl.BlockSpec((rows, BLOCK), lambda i: (i, 0)),
        out_shape=jax.ShapeDtypeStruct((count, BLOCK), F32),
        compiler_params=pltpu.CompilerParams(vmem_limit_bytes=VMEM_LIMIT),
        cost_estimate=cost(count),
    )(pltpu.with_memory_space_constraint(slab, pltpu.HBM), rot)


def staying(slab, rot, rows=512):
    count = slab.shape[0]
    return pl.pallas_call(
        rotate_kernel,
        grid=(count // rows,),
        in_specs=[
            pl.BlockSpec((rows, WIDTH), lambda i: (i, 0)),
            pl.BlockSpec((WIDTH, WIDTH), lambda i: (0, 0)),
        ],
        out_specs=pl.BlockSpec((rows, BLOCK), lambda i: (i, 0)),
        out_shape=pltpu.HBM((count, WIDTH), F32),
        compiler_params=pltpu.CompilerParams(vmem_limit_bytes=VMEM_LIMIT),
        cost_estimate=cost(count),
    )(pltpu.with_memory_space_constraint(slab, pltpu.HBM), rot)


def raw_kernel(x_ref, p0_ref, p1_ref, p2_ref, p3_ref, _, out_ref, full, rot):
    @pl.when(pl.program_id(0) == 0)
    def _():
        for d, piece in enumerate((p0_ref, p1_ref, p2_ref, p3_ref)):
            core, x, y = place()
            for n in range(8):
                start = ((4 * (y ^ d) + (x ^ (n >> 1))) * 2 + (core ^ (n & 1))) * 8
                full[pl.ds(pl.multiple_of(start, 8), 8), :] = piece[8 * n : 8 * n + 8, :]
        high = full[...].astype(BF16)
        rot[:, 0:128] = high
        rot[:, 128:256] = (full[...] - high.astype(F32)).astype(BF16)

    out_ref[...] = rotation(x_ref[...], rot[...])


def rotated_raw(raw, pieces, result, rows=RAW // 4):
    count = raw.shape[0]
    piece = pl.BlockSpec((64, BLOCK), lambda i: (0, 0))
    return pl.pallas_call(
        raw_kernel,
        grid=(count // rows,),
        in_specs=[
            pl.BlockSpec((rows, WIDTH), lambda i: (i, 0)),
            piece,
            piece,
            piece,
            piece,
            pl.BlockSpec(memory_space=pl.ANY),
        ],
        out_specs=pl.BlockSpec((rows, BLOCK), lambda i: (i, 1)),
        out_shape=pltpu.HBM(result.shape, F32),
        scratch_shapes=[pltpu.VMEM((WIDTH, BLOCK), F32), pltpu.VMEM((WIDTH, WIDTH), BF16)],
        input_output_aliases={5: 0},
        compiler_params=pltpu.CompilerParams(vmem_limit_bytes=VMEM_LIMIT),
        cost_estimate=cost(count),
    )(raw, *pieces, result)


def per_device(slab, block_ids):
    core, _, _ = place()
    parts, raw = summed_over_rows(local_gram(slab), core, slab[:RAW])
    first, rot_leave, rot_stay, diag = rounds_and_first_chunk(parts, slab, block_ids)
    first, raw = lax.optimization_barrier((first, raw))
    arrived = [passed_along(first)]
    extra = arrived[0][CHUNKS[0] :]
    starts = [RAW + sum(CHUNKS[:n]) for n in range(len(CHUNKS))]
    for start, count in zip(starts[1:], CHUNKS[1:]):
        arrived.append(passed_along(leaving(slab, rot_leave, start, count)))
    new_slab = staying(slab, rot_stay)
    both = jnp.concatenate([extra[:8], exchanged(extra[:8], 1)])
    eight = jnp.concatenate(with_three_others(both, 1))
    new_slab = rotated_raw(raw, with_three_others(eight, 3), new_slab)
    for start, count, chunk in zip(starts, CHUNKS, arrived):
        new_slab = lax.dynamic_update_slice(new_slab, chunk[:count], (start, BLOCK))
    total_rows = slab.shape[0] * lax.axis_size("row")
    squares = jnp.concatenate([diag[0, :BLOCK], extra[8]])
    col_norms = jnp.sqrt(jnp.maximum(squares, 0.0) / total_rows)
    new_ids = jnp.stack([jnp.min(block_ids), extra[12, 0].astype(jnp.int32)])
    return (new_slab, col_norms, new_ids)


def solution(mesh):
    return jax.shard_map(
        per_device,
        mesh=mesh,
        in_specs=(P("row", "pair"), P("pair")),
        out_specs=(P("row", "pair"), P("pair"), P("pair")),
        check_vma=False,
    )
```

```python
import functools

import jax
import jax.numpy as jnp
import numpy as np
from jax import lax
from jax.experimental import pallas as pl
from jax.experimental.pallas import tpu as pltpu
from jax.sharding import PartitionSpec as P

ROUNDS = 48
BLOCK = 128
WIDTH = 256
F32 = jnp.float32
BF16 = jnp.bfloat16
HIGHEST = lax.Precision.HIGHEST
VMEM_LIMIT = 32 * 1024 * 1024
ROWS = 4096
RAW = 512
CHUNKS = (1536 - RAW, 2304, 256)
EXTRA = 16
PIECES = 4
STEP = CHUNKS[0] // PIECES
PACKED = 272
PARTS = 4


def product(a, b):
    return jnp.dot(a, b, preferred_element_type=F32)


def product_over_rows(a, b):
    return lax.dot_general(a, b, (((0,), (0,)), ((), ())), preferred_element_type=F32)


def gram_kernel(slab_ref, out_ref, x_ref, even, odd, sems):
    rows = ROWS // PARTS
    parts = [pl.ds(n * rows, rows) for n in range(PARTS)]
    copies = [
        pltpu.make_async_copy(slab_ref.at[part, :], x_ref.at[part, :], sems.at[n])
        for n, part in enumerate(parts)
    ]
    for copy in copies:
        copy.start()
    for n, part in enumerate(parts):
        copies[n].wait()
        x = x_ref[part, :]
        high = x.astype(BF16)
        rest = x - high.astype(F32)
        mid = rest.astype(BF16)
        low = (rest - mid.astype(F32)).astype(BF16)
        same = product_over_rows(high, high) + product_over_rows(mid, mid)
        cross = product_over_rows(high, mid) + product_over_rows(high, low)
        even[...] = same if n == 0 else even[...] + same
        odd[...] = cross if n == 0 else odd[...] + cross
    gram = even[...] + odd[...] + odd[...].T
    row = lax.broadcasted_iota(jnp.int32, (BLOCK, BLOCK), 0)
    col = lax.broadcasted_iota(jnp.int32, (BLOCK, BLOCK), 1)
    last = gram[128:256, 128:256]
    out_ref[0:128, :] = jnp.where(row <= col, gram[0:128, 0:128], last)
    out_ref[128:256, :] = gram[0:128, 128:256]
    diag = jnp.sum(jnp.where(row == col, last, 0.0), axis=0, keepdims=True)
    out_ref[256:272, :] = jnp.broadcast_to(diag, (16, BLOCK))


def local_gram(slab):
    return pl.pallas_call(
        gram_kernel,
        in_specs=[pl.BlockSpec(memory_space=pl.ANY)],
        out_specs=pl.BlockSpec(memory_space=pltpu.VMEM),
        out_shape=jax.ShapeDtypeStruct((PACKED, BLOCK), F32),
        scratch_shapes=[
            pltpu.VMEM((ROWS, WIDTH), F32),
            pltpu.VMEM((WIDTH, WIDTH), F32),
            pltpu.VMEM((WIDTH, WIDTH), F32),
            pltpu.SemaphoreType.DMA((PARTS,)),
        ],
        compiler_params=pltpu.CompilerParams(vmem_limit_bytes=VMEM_LIMIT),
    )(pltpu.with_memory_space_constraint(slab, pltpu.HBM))


def place():
    me = lax.axis_index("row")
    return me & 1, (me >> 1) & 3, (me >> 3) & 3


def exchanged(array, mask):
    return lax.ppermute(array, "row", [(i, i ^ mask) for i in range(128)])


def passed_along(array):
    return lax.ppermute(array, "pair", [(0, 1), (1, 0)])


def with_three_others(mine, shift):
    return [mine] + [exchanged(mine, d << shift) for d in (1, 2, 3)]


def summed_over_four(mine, shift):
    parts = with_three_others(mine, shift)
    return (parts[0] + parts[2]) + (parts[1] + parts[3])


def summed_over_rows(part, core, raw):
    half = part.shape[0] // 2
    mine = lax.dynamic_slice_in_dim(part, core * half, half, 0)
    yours = lax.dynamic_slice_in_dim(part, (1 - core) * half, half, 0)
    total = summed_over_four(mine + exchanged(yours, 1), 5)
    raw, total = lax.optimization_barrier((raw, total))
    raw = passed_along(raw)
    total = summed_over_four(total, 3)
    total = summed_over_four(total, 1)
    return (total, exchanged(total, 1)), raw


def meetings(step):
    ring = WIDTH - 1
    return [(step, ring)] + [((step + k) % ring, (step - k) % ring) for k in range(1, BLOCK)]


def round_tables():
    top, bottom = np.arange(BLOCK), WIDTH - 1 - np.arange(BLOCK)
    table = np.zeros((ROUNDS, 8, BLOCK), np.int32)
    table[:, 0] = np.arange(BLOCK)
    for step in range(ROUNDS):
        first = {i for i, _ in meetings(step)}
        table[step, 2] = [t in first for t in top]
        if step == ROUNDS - 1:
            break
        now, later = np.zeros(WIDTH, int), np.zeros(WIDTH, int)
        for pairs, partner in ((meetings(step), now), (meetings(step + 1), later)):
            for i, j in pairs:
                partner[i], partner[j] = j, i
        side = np.full(WIDTH, -1)
        for member in range(WIDTH):
            while side[member] < 0:
                side[member], side[now[member]] = 0, 1
                member = later[now[member]]
        swap = side[top] == 1
        table[step, 1] = swap
        top, bottom = np.where(swap, bottom, top), np.where(swap, top, bottom)
        lane = np.zeros(WIDTH, int)
        lane[bottom] = np.arange(BLOCK)
        table[step, 0] = lane[later[top]]
        bottom = later[top]
    last = np.concatenate([top, bottom]).astype(np.int32)
    return table, np.repeat(last[:, None], BLOCK, axis=1)


def angles(g, d_top, d_bot, top_first):
    diff = d_bot - d_top
    double = jnp.where((diff > 0) | ((diff == 0) & top_first), 2.0 * g, -2.0 * g)
    den = jnp.abs(diff) + jnp.sqrt(diff * diff + 4.0 * g * g)
    tang = jnp.where(den > 0, double / jnp.where(den > 0, den, 1.0), 0.0)
    cosv = lax.rsqrt(1.0 + tang * tang)
    return tang, cosv, tang * cosv


def rounds_kernel(
    ids_ref, table_ref, last_ref, mine_ref, other_ref, slab_ref, first_ref, leave_ref, stay_ref, diag_ref,
    packed, vt, vb, wt, wb, start_ref, x_ref, sem,
):
    fetch = pltpu.make_async_copy(slab_ref.at[pl.ds(RAW, CHUNKS[0]), :], x_ref, sem)
    fetch.start()
    core, x, y = place()
    swap_blocks = (ids_ref[1] <= ids_ref[0]).astype(jnp.int32)
    for h, part in enumerate((mine_ref, other_ref)):
        start = pl.multiple_of((core ^ h) * (PACKED // 2), 8)
        packed[pl.ds(start, PACKED // 2), :] = part[...]
    half = BLOCK
    row = lax.broadcasted_iota(jnp.int32, (2 * half, half), 0)
    col = lax.broadcasted_iota(jnp.int32, (2 * half, half), 1)
    vt[...] = (row == col).astype(F32)
    vb[...] = (row == 255 - col).astype(F32)
    both, b = packed[0:128, :], packed[128:256, :]
    mirrored = both.T
    above, below = row[:half] < col[:half], row[:half] > col[:half]
    a = jnp.where(below, mirrored, both)
    c = jnp.where(below, both, jnp.where(above, mirrored, packed[256:257, :]))
    both, b = packed[0:128, :], packed[128:256, :]
    mirrored = both.T
    above, below = row[:half] < col[:half], row[:half] > col[:half]
    a = jnp.where(below, mirrored, both)
    c = jnp.where(below, both, jnp.where(above, mirrored, packed[256:257, :]))
    rev = (row[:half] == half - 1 - col[:half]).astype(F32)
    wt[0:128, :] = a
    wt[128:256, :] = b.T
    turned = half - 1 - lax.broadcasted_iota(jnp.int32, (8, half), 1)
    for n, part in enumerate((b, c)):
        for k in range(0, half, 8):
            wb[half * n + k : half * n + k + 8, :] = jnp.take_along_axis(
                part[k : k + 8, :], turned, axis=1, mode="promise_in_bounds"
            )
    eye = row[:half] == col[:half]
    d_top = jnp.sum(jnp.where(eye, wt[0:128, :], 0.0), axis=0, keepdims=True)
    anti = row[:half] == half - 1 - col[:half]
    d_bot = jnp.sum(jnp.where(anti, wb[128:256, :], 0.0), axis=0, keepdims=True)
    g = (jnp.sum(jnp.where(eye, wb[0:128, :], 0.0), axis=0, keepdims=True))
    for n, v in enumerate((g, d_top, d_bot)):
        start_ref[n] = jnp.broadcast_to(v, (8, half))

    def one_round(step, state):
        g, d_top, d_bot = state
        source, swap, top_first = (
            jnp.broadcast_to(table_ref[step, n : n + 1, :], (8, half)) for n in range(3)
        )
        swap = swap > 0

        def moved(bottom):
            return jnp.take_along_axis(bottom, source, axis=1, mode="promise_in_bounds")

        t, c, s = angles(g, d_top, d_bot, top_first > 0)
        a, b = d_top - t * g, d_bot + t * g
        d_top, d_bot = jnp.where(swap, b, a), moved(jnp.where(swap, a, b))
        top_a, top_b = jnp.where(swap, s, c), jnp.where(swap, c, -s)
        bot_a, bot_b = jnp.where(swap, c, s), jnp.where(swap, -s, c)
        acc = [jnp.zeros((8, half), F32) for _ in range(4)]
        for k in range(32):
            sl = pl.ds(8 * k, 8)
            a, b = vt[sl, :], vb[sl, :]
            new_vt = top_a * a + top_b * b
            vt[sl, :] = new_vt
            vb[sl, :] = moved(bot_a * a + bot_b * b)
            a, b = wt[sl, :], wb[sl, :]
            wt[sl, :] = top_a * a + top_b * b
            new_wb = moved(bot_a * a + bot_b * b)
            wb[sl, :] = new_wb
            acc[k % 4] = acc[k % 4] + new_vt * new_wb
        g = jnp.sum((acc[0] + acc[1]) + (acc[2] + acc[3]), axis=0, keepdims=True)
        return jnp.broadcast_to(g, (8, half)), d_top, d_bot

    g, d_top, d_bot = lax.fori_loop(0, ROUNDS, one_round, tuple(start_ref[n] for n in range(3)))
    dot = functools.partial(jnp.dot, precision=HIGHEST, preferred_element_type=F32)
    lane = lax.broadcasted_iota(jnp.int32, (half, half), 1)
    parts = []
    for ref in (vt, vb):
        high = ref[...].astype(BF16)
        parts.append((high, (ref[...] - high.astype(F32)).astype(BF16)))
    diags = []
    for n, out_ref in enumerate((stay_ref, leave_ref)):
        column = lane + half * (n ^ swap_blocks)
        p_top = (last_ref[0:half, :] == column).astype(F32)
        p_bot = (last_ref[half : 2 * half, :] == column).astype(F32)
        for m in range(2):
            part = product(parts[0][m], p_top.astype(BF16)) + product(parts[1][m], p_bot.astype(BF16))
            out_ref[:, half * m : half * m + half] = part.astype(BF16)
        diags.append(dot(d_top, p_top) + dot(d_bot, p_bot))
    diag = jnp.concatenate(diags, axis=1)
    diag_ref[...] = diag
    wt[...] = leave_ref[:, 0:128].astype(F32) + leave_ref[:, 128:256].astype(F32)
    piece = pl.ds(pl.multiple_of(((4 * y + x) * 2 + core) * 8, 8), 8)
    first_ref[CHUNKS[0] : CHUNKS[0] + 8, :] = wt[piece, :]
    label = jnp.full((8, half), jnp.maximum(ids_ref[0], ids_ref[1]).astype(F32))
    upper = lax.broadcasted_iota(jnp.int32, (8, half), 0) < 4
    first_ref[CHUNKS[0] + 8 : CHUNKS[0] + 16, :] = jnp.where(upper, diag[:, 128:256], label)
    fetch.wait()
    for start in range(0, CHUNKS[0], STEP):
        first_ref[start : start + STEP, :] = rotation(x_ref[start : start + STEP, :], leave_ref[...])


def rotation(x, rot):
    high = x.astype(BF16)
    low = (x - high.astype(F32)).astype(BF16)
    both = product(high, rot)
    return (both[:, 0:128] + both[:, 128:256]) + product(low, rot[:, 0:128])


def rounds_and_first_chunk(parts, slab, block_ids):
    in_vmem = pl.BlockSpec(memory_space=pltpu.VMEM)
    return pl.pallas_call(
        rounds_kernel,
        in_specs=[
            pl.BlockSpec(memory_space=pltpu.SMEM),
            in_vmem,
            in_vmem,
            in_vmem,
            in_vmem,
            pl.BlockSpec(memory_space=pl.ANY),
        ],
        out_specs=(in_vmem,) * 4,
        out_shape=(
            jax.ShapeDtypeStruct((CHUNKS[0] + EXTRA, BLOCK), F32),
            jax.ShapeDtypeStruct((WIDTH, WIDTH), BF16),
            jax.ShapeDtypeStruct((WIDTH, WIDTH), BF16),
            jax.ShapeDtypeStruct((8, WIDTH), F32),
        ),
        scratch_shapes=[pltpu.VMEM((PACKED, BLOCK), F32)]
        + [pltpu.VMEM((WIDTH, BLOCK), F32)] * 4
        + [
            pltpu.VMEM((3, 8, BLOCK), F32),
            pltpu.VMEM((CHUNKS[0], WIDTH), F32),
            pltpu.SemaphoreType.DMA,
        ],
        compiler_params=pltpu.CompilerParams(vmem_limit_bytes=VMEM_LIMIT),
        cost_estimate=pl.CostEstimate(flops=0, bytes_accessed=0, transcendentals=0),
    )(block_ids, *(jnp.asarray(t) for t in round_tables()), *parts, pltpu.with_memory_space_constraint(slab, pltpu.HBM))


def cost(count):
    return pl.CostEstimate(
        flops=6 * count * WIDTH * BLOCK, bytes_accessed=6 * count * WIDTH, transcendentals=0
    )


def rotate_kernel(x_ref, rot_ref, out_ref):
    out_ref[...] = rotation(x_ref[...], rot_ref[...])


def leaving(slab, rot, first, count, rows=256):
    return pl.pallas_call(
        rotate_kernel,
        grid=(count // rows,),
        in_specs=[
            pl.BlockSpec((rows, WIDTH), lambda i: (i + first // rows, 0)),
            pl.BlockSpec((WIDTH, WIDTH), lambda i: (0, 0)),
        ],
        out_specs=pl.BlockSpec((rows, BLOCK), lambda i: (i, 0)),
        out_shape=jax.ShapeDtypeStruct((count, BLOCK), F32),
        compiler_params=pltpu.CompilerParams(vmem_limit_bytes=VMEM_LIMIT),
        cost_estimate=cost(count),
    )(pltpu.with_memory_space_constraint(slab, pltpu.HBM), rot)


def staying(slab, rot, rows=512):
    count = slab.shape[0]
    return pl.pallas_call(
        rotate_kernel,
        grid=(count // rows,),
        in_specs=[
            pl.BlockSpec((rows, WIDTH), lambda i: (i, 0)),
            pl.BlockSpec((WIDTH, WIDTH), lambda i: (0, 0)),
        ],
        out_specs=pl.BlockSpec((rows, BLOCK), lambda i: (i, 0)),
        out_shape=pltpu.HBM((count, WIDTH), F32),
        compiler_params=pltpu.CompilerParams(vmem_limit_bytes=VMEM_LIMIT),
        cost_estimate=cost(count),
    )(pltpu.with_memory_space_constraint(slab, pltpu.HBM), rot)


def raw_kernel(x_ref, p0_ref, p1_ref, p2_ref, p3_ref, _, out_ref, full, rot):
    @pl.when(pl.program_id(0) == 0)
    def _():
        for d, piece in enumerate((p0_ref, p1_ref, p2_ref, p3_ref)):
            core, x, y = place()
            for n in range(8):
                start = ((4 * (y ^ d) + (x ^ (n >> 1))) * 2 + (core ^ (n & 1))) * 8
                full[pl.ds(pl.multiple_of(start, 8), 8), :] = piece[8 * n : 8 * n + 8, :]
        high = full[...].astype(BF16)
        rot[:, 0:128] = high
        rot[:, 128:256] = (full[...] - high.astype(F32)).astype(BF16)

    out_ref[...] = rotation(x_ref[...], rot[...])


def rotated_raw(raw, pieces, result, rows=RAW // PIECES):
    count = raw.shape[0]
    piece = pl.BlockSpec((64, BLOCK), lambda i: (0, 0))
    return pl.pallas_call(
        raw_kernel,
        grid=(count // rows,),
        in_specs=[
            pl.BlockSpec((rows, WIDTH), lambda i: (i, 0)),
            piece,
            piece,
            piece,
            piece,
            pl.BlockSpec(memory_space=pl.ANY),
        ],
        out_specs=pl.BlockSpec((rows, BLOCK), lambda i: (i, 1)),
        out_shape=pltpu.HBM(result.shape, F32),
        scratch_shapes=[pltpu.VMEM((WIDTH, BLOCK), F32), pltpu.VMEM((WIDTH, WIDTH), BF16)],
        input_output_aliases={5: 0},
        compiler_params=pltpu.CompilerParams(vmem_limit_bytes=VMEM_LIMIT),
        cost_estimate=cost(count),
    )(raw, *pieces, result)


def per_device(slab, block_ids):
    core, _, _ = place()
    parts, raw = summed_over_rows(local_gram(slab), core, slab[:RAW])
    first, rot_leave, rot_stay, diag = rounds_and_first_chunk(parts, slab, block_ids)
    first, raw = lax.optimization_barrier((first, raw))
    arrived = [passed_along(first)]
    extra = arrived[0][CHUNKS[0] :]
    starts = [RAW + sum(CHUNKS[:n]) for n in range(len(CHUNKS))]
    for start, count in zip(starts[1:], CHUNKS[1:]):
        arrived.append(passed_along(leaving(slab, rot_leave, start, count)))
    new_slab = staying(slab, rot_stay)
    both = jnp.concatenate([extra[:8], exchanged(extra[:8], 1)])
    eight = jnp.concatenate(with_three_others(both, 1))
    new_slab = rotated_raw(raw, with_three_others(eight, 3), new_slab)
    for start, count, chunk in zip(starts, CHUNKS, arrived):
        new_slab = lax.dynamic_update_slice(new_slab, chunk[:count], (start, BLOCK))
    total_rows = slab.shape[0] * lax.axis_size("row")
    squares = jnp.concatenate([diag[0, :BLOCK], extra[8]])
    col_norms = jnp.sqrt(jnp.maximum(squares, 0.0) / total_rows)
    new_ids = jnp.stack([jnp.min(block_ids), extra[12, 0].astype(jnp.int32)])
    return (new_slab, col_norms, new_ids)


def solution(mesh):
    return jax.shard_map(
        per_device,
        mesh=mesh,
        in_specs=(P("row", "pair"), P("pair")),
        out_specs=(P("row", "pair"), P("pair"), P("pair")),
        check_vma=False,
    )
```

```python
import functools

import jax
import jax.numpy as jnp
import numpy as np
from jax import lax
from jax.experimental import pallas as pl
from jax.experimental.pallas import tpu as pltpu
from jax.sharding import PartitionSpec as P

ROUNDS = 48
BLOCK = 128
WIDTH = 256
F32 = jnp.float32
BF16 = jnp.bfloat16
HIGHEST = lax.Precision.HIGHEST
VMEM_LIMIT = 32 * 1024 * 1024
ROWS = 4096
RAW = 512
CHUNKS = (1536 - RAW, 2304, 256)
EXTRA = 16
PIECES = 4
STEP = CHUNKS[0] // PIECES
PACKED = 272
PARTS = (512, 1024, 1280, 1280)


def product(a, b):
    return jnp.dot(a, b, preferred_element_type=F32)


def product_over_rows(a, b):
    return lax.dot_general(a, b, (((0,), (0,)), ((), ())), preferred_element_type=F32)


def gram_kernel(slab_ref, out_ref, x_ref, even, odd, sems):
    parts = [pl.ds(sum(PARTS[:n]), rows) for n, rows in enumerate(PARTS)]
    copies = [
        pltpu.make_async_copy(slab_ref.at[part, :], x_ref.at[part, :], sems.at[n])
        for n, part in enumerate(parts)
    ]
    for copy in copies:
        copy.start()
    for n, part in enumerate(parts):
        copies[n].wait()
        x = x_ref[part, :]
        high = x.astype(BF16)
        rest = x - high.astype(F32)
        mid = rest.astype(BF16)
        low = (rest - mid.astype(F32)).astype(BF16)
        same = product_over_rows(high, high) + product_over_rows(mid, mid)
        cross = product_over_rows(high, mid) + product_over_rows(high, low)
        even[...] = same if n == 0 else even[...] + same
        odd[...] = cross if n == 0 else odd[...] + cross
    gram = even[...] + odd[...] + odd[...].T
    row = lax.broadcasted_iota(jnp.int32, (BLOCK, BLOCK), 0)
    col = lax.broadcasted_iota(jnp.int32, (BLOCK, BLOCK), 1)
    last = gram[128:256, 128:256]
    out_ref[0:128, :] = jnp.where(row <= col, gram[0:128, 0:128], last)
    out_ref[128:256, :] = gram[0:128, 128:256]
    diag = jnp.sum(jnp.where(row == col, last, 0.0), axis=0, keepdims=True)
    out_ref[256:272, :] = jnp.broadcast_to(diag, (16, BLOCK))


def local_gram(slab):
    return pl.pallas_call(
        gram_kernel,
        in_specs=[pl.BlockSpec(memory_space=pl.ANY)],
        out_specs=pl.BlockSpec(memory_space=pltpu.VMEM),
        out_shape=jax.ShapeDtypeStruct((PACKED, BLOCK), F32),
        scratch_shapes=[
            pltpu.VMEM((ROWS, WIDTH), F32),
            pltpu.VMEM((WIDTH, WIDTH), F32),
            pltpu.VMEM((WIDTH, WIDTH), F32),
            pltpu.SemaphoreType.DMA((len(PARTS),)),
        ],
        compiler_params=pltpu.CompilerParams(vmem_limit_bytes=VMEM_LIMIT),
    )(pltpu.with_memory_space_constraint(slab, pltpu.HBM))


def place():
    me = lax.axis_index("row")
    return me & 1, (me >> 1) & 3, (me >> 3) & 3


def exchanged(array, mask):
    return lax.ppermute(array, "row", [(i, i ^ mask) for i in range(128)])


def passed_along(array):
    return lax.ppermute(array, "pair", [(0, 1), (1, 0)])


def with_three_others(mine, shift):
    return [mine] + [exchanged(mine, d << shift) for d in (1, 2, 3)]


def summed_over_four(mine, shift):
    parts = with_three_others(mine, shift)
    return (parts[0] + parts[2]) + (parts[1] + parts[3])


def summed_over_rows(part, core, raw):
    half = part.shape[0] // 2
    mine = lax.dynamic_slice_in_dim(part, core * half, half, 0)
    yours = lax.dynamic_slice_in_dim(part, (1 - core) * half, half, 0)
    total = summed_over_four(mine + exchanged(yours, 1), 5)
    raw, total = lax.optimization_barrier((raw, total))
    raw = passed_along(raw)
    total = summed_over_four(total, 3)
    total = summed_over_four(total, 1)
    return (total, exchanged(total, 1)), raw


def meetings(step):
    ring = WIDTH - 1
    return [(step, ring)] + [((step + k) % ring, (step - k) % ring) for k in range(1, BLOCK)]


def round_tables():
    top, bottom = np.arange(BLOCK), WIDTH - 1 - np.arange(BLOCK)
    table = np.zeros((ROUNDS, 8, BLOCK), np.int32)
    table[:, 0] = np.arange(BLOCK)
    for step in range(ROUNDS):
        first = {i for i, _ in meetings(step)}
        table[step, 2] = [t in first for t in top]
        if step == ROUNDS - 1:
            break
        now, later = np.zeros(WIDTH, int), np.zeros(WIDTH, int)
        for pairs, partner in ((meetings(step), now), (meetings(step + 1), later)):
            for i, j in pairs:
                partner[i], partner[j] = j, i
        side = np.full(WIDTH, -1)
        for member in range(WIDTH):
            while side[member] < 0:
                side[member], side[now[member]] = 0, 1
                member = later[now[member]]
        swap = side[top] == 1
        table[step, 1] = swap
        top, bottom = np.where(swap, bottom, top), np.where(swap, top, bottom)
        lane = np.zeros(WIDTH, int)
        lane[bottom] = np.arange(BLOCK)
        table[step, 0] = lane[later[top]]
        bottom = later[top]
    last = np.concatenate([top, bottom]).astype(np.int32)
    return table, np.repeat(last[:, None], BLOCK, axis=1)


def angles(g, d_top, d_bot, top_first):
    diff = d_bot - d_top
    double = jnp.where((diff > 0) | ((diff == 0) & top_first), 2.0 * g, -2.0 * g)
    den = jnp.abs(diff) + jnp.sqrt(diff * diff + 4.0 * g * g)
    tang = jnp.where(den > 0, double / jnp.where(den > 0, den, 1.0), 0.0)
    cosv = lax.rsqrt(1.0 + tang * tang)
    return tang, cosv, tang * cosv


def rounds_kernel(
    ids_ref, table_ref, last_ref, mine_ref, other_ref, slab_ref, first_ref, leave_ref, stay_ref, diag_ref,
    packed, vt, vb, wt, wb, start_ref, x_ref, sem,
):
    fetch = pltpu.make_async_copy(slab_ref.at[pl.ds(RAW, CHUNKS[0]), :], x_ref, sem)
    fetch.start()
    core, x, y = place()
    swap_blocks = (ids_ref[1] <= ids_ref[0]).astype(jnp.int32)
    for h, part in enumerate((mine_ref, other_ref)):
        start = pl.multiple_of((core ^ h) * (PACKED // 2), 8)
        packed[pl.ds(start, PACKED // 2), :] = part[...]
    half = BLOCK
    row = lax.broadcasted_iota(jnp.int32, (2 * half, half), 0)
    col = lax.broadcasted_iota(jnp.int32, (2 * half, half), 1)
    vt[...] = (row == col).astype(F32)
    vb[...] = (row == 255 - col).astype(F32)
    both, b = packed[0:128, :], packed[128:256, :]
    mirrored = both.T
    above, below = row[:half] < col[:half], row[:half] > col[:half]
    a = jnp.where(below, mirrored, both)
    c = jnp.where(below, both, jnp.where(above, mirrored, packed[256:257, :]))
    both, b = packed[0:128, :], packed[128:256, :]
    mirrored = both.T
    above, below = row[:half] < col[:half], row[:half] > col[:half]
    a = jnp.where(below, mirrored, both)
    c = jnp.where(below, both, jnp.where(above, mirrored, packed[256:257, :]))
    rev = (row[:half] == half - 1 - col[:half]).astype(F32)
    wt[0:128, :] = a
    wt[128:256, :] = b.T
    turned = half - 1 - lax.broadcasted_iota(jnp.int32, (8, half), 1)
    for n, part in enumerate((b, c)):
        for k in range(0, half, 8):
            wb[half * n + k : half * n + k + 8, :] = jnp.take_along_axis(
                part[k : k + 8, :], turned, axis=1, mode="promise_in_bounds"
            )
    eye = row[:half] == col[:half]
    d_top = jnp.sum(jnp.where(eye, wt[0:128, :], 0.0), axis=0, keepdims=True)
    anti = row[:half] == half - 1 - col[:half]
    d_bot = jnp.sum(jnp.where(anti, wb[128:256, :], 0.0), axis=0, keepdims=True)
    g = (jnp.sum(jnp.where(eye, wb[0:128, :], 0.0), axis=0, keepdims=True))
    for n, v in enumerate((g, d_top, d_bot)):
        start_ref[n] = jnp.broadcast_to(v, (8, half))

    def one_round(step, state):
        g, d_top, d_bot = state
        source, swap, top_first = (
            jnp.broadcast_to(table_ref[step, n : n + 1, :], (8, half)) for n in range(3)
        )
        swap = swap > 0

        def moved(bottom):
            return jnp.take_along_axis(bottom, source, axis=1, mode="promise_in_bounds")

        t, c, s = angles(g, d_top, d_bot, top_first > 0)
        a, b = d_top - t * g, d_bot + t * g
        d_top, d_bot = jnp.where(swap, b, a), moved(jnp.where(swap, a, b))
        top_a, top_b = jnp.where(swap, s, c), jnp.where(swap, c, -s)
        bot_a, bot_b = jnp.where(swap, c, s), jnp.where(swap, -s, c)
        acc = [jnp.zeros((8, half), F32) for _ in range(4)]
        for k in range(32):
            sl = pl.ds(8 * k, 8)
            a, b = vt[sl, :], vb[sl, :]
            new_vt = top_a * a + top_b * b
            vt[sl, :] = new_vt
            vb[sl, :] = moved(bot_a * a + bot_b * b)
            a, b = wt[sl, :], wb[sl, :]
            wt[sl, :] = top_a * a + top_b * b
            new_wb = moved(bot_a * a + bot_b * b)
            wb[sl, :] = new_wb
            acc[k % 4] = acc[k % 4] + new_vt * new_wb
        g = jnp.sum((acc[0] + acc[1]) + (acc[2] + acc[3]), axis=0, keepdims=True)
        return jnp.broadcast_to(g, (8, half)), d_top, d_bot

    g, d_top, d_bot = lax.fori_loop(0, ROUNDS, one_round, tuple(start_ref[n] for n in range(3)))
    dot = functools.partial(jnp.dot, precision=HIGHEST, preferred_element_type=F32)
    lane = lax.broadcasted_iota(jnp.int32, (half, half), 1)
    parts = []
    for ref in (vt, vb):
        high = ref[...].astype(BF16)
        parts.append((high, (ref[...] - high.astype(F32)).astype(BF16)))
    diags = []
    for n, out_ref in enumerate((stay_ref, leave_ref)):
        column = lane + half * (n ^ swap_blocks)
        p_top = (last_ref[0:half, :] == column).astype(F32)
        p_bot = (last_ref[half : 2 * half, :] == column).astype(F32)
        for m in range(2):
            part = product(parts[0][m], p_top.astype(BF16)) + product(parts[1][m], p_bot.astype(BF16))
            out_ref[:, half * m : half * m + half] = part.astype(BF16)
        diags.append(dot(d_top, p_top) + dot(d_bot, p_bot))
    diag = jnp.concatenate(diags, axis=1)
    diag_ref[...] = diag
    wt[...] = leave_ref[:, 0:128].astype(F32) + leave_ref[:, 128:256].astype(F32)
    piece = pl.ds(pl.multiple_of(((4 * y + x) * 2 + core) * 8, 8), 8)
    first_ref[CHUNKS[0] : CHUNKS[0] + 8, :] = wt[piece, :]
    label = jnp.full((8, half), jnp.maximum(ids_ref[0], ids_ref[1]).astype(F32))
    upper = lax.broadcasted_iota(jnp.int32, (8, half), 0) < 4
    first_ref[CHUNKS[0] + 8 : CHUNKS[0] + 16, :] = jnp.where(upper, diag[:, 128:256], label)
    fetch.wait()
    for start in range(0, CHUNKS[0], STEP):
        first_ref[start : start + STEP, :] = rotation(x_ref[start : start + STEP, :], leave_ref[...])


def rotation(x, rot):
    high = x.astype(BF16)
    low = (x - high.astype(F32)).astype(BF16)
    both = product(high, rot)
    return (both[:, 0:128] + both[:, 128:256]) + product(low, rot[:, 0:128])


def rounds_and_first_chunk(parts, slab, block_ids):
    in_vmem = pl.BlockSpec(memory_space=pltpu.VMEM)
    return pl.pallas_call(
        rounds_kernel,
        in_specs=[
            pl.BlockSpec(memory_space=pltpu.SMEM),
            in_vmem,
            in_vmem,
            in_vmem,
            in_vmem,
            pl.BlockSpec(memory_space=pl.ANY),
        ],
        out_specs=(in_vmem,) * 4,
        out_shape=(
            jax.ShapeDtypeStruct((CHUNKS[0] + EXTRA, BLOCK), F32),
            jax.ShapeDtypeStruct((WIDTH, WIDTH), BF16),
            jax.ShapeDtypeStruct((WIDTH, WIDTH), BF16),
            jax.ShapeDtypeStruct((8, WIDTH), F32),
        ),
        scratch_shapes=[pltpu.VMEM((PACKED, BLOCK), F32)]
        + [pltpu.VMEM((WIDTH, BLOCK), F32)] * 4
        + [
            pltpu.VMEM((3, 8, BLOCK), F32),
            pltpu.VMEM((CHUNKS[0], WIDTH), F32),
            pltpu.SemaphoreType.DMA,
        ],
        compiler_params=pltpu.CompilerParams(vmem_limit_bytes=VMEM_LIMIT),
        cost_estimate=pl.CostEstimate(flops=0, bytes_accessed=0, transcendentals=0),
    )(block_ids, *(jnp.asarray(t) for t in round_tables()), *parts, pltpu.with_memory_space_constraint(slab, pltpu.HBM))


def cost(count):
    return pl.CostEstimate(
        flops=6 * count * WIDTH * BLOCK, bytes_accessed=6 * count * WIDTH, transcendentals=0
    )


def rotate_kernel(x_ref, rot_ref, out_ref):
    out_ref[...] = rotation(x_ref[...], rot_ref[...])


def leaving(slab, rot, first, count, rows=256):
    return pl.pallas_call(
        rotate_kernel,
        grid=(count // rows,),
        in_specs=[
            pl.BlockSpec((rows, WIDTH), lambda i: (i + first // rows, 0)),
            pl.BlockSpec((WIDTH, WIDTH), lambda i: (0, 0)),
        ],
        out_specs=pl.BlockSpec((rows, BLOCK), lambda i: (i, 0)),
        out_shape=jax.ShapeDtypeStruct((count, BLOCK), F32),
        compiler_params=pltpu.CompilerParams(vmem_limit_bytes=VMEM_LIMIT),
        cost_estimate=cost(count),
    )(pltpu.with_memory_space_constraint(slab, pltpu.HBM), rot)


def staying(slab, rot, rows=512):
    count = slab.shape[0]
    return pl.pallas_call(
        rotate_kernel,
        grid=(count // rows,),
        in_specs=[
            pl.BlockSpec((rows, WIDTH), lambda i: (i, 0)),
            pl.BlockSpec((WIDTH, WIDTH), lambda i: (0, 0)),
        ],
        out_specs=pl.BlockSpec((rows, BLOCK), lambda i: (i, 0)),
        out_shape=pltpu.HBM((count, WIDTH), F32),
        compiler_params=pltpu.CompilerParams(vmem_limit_bytes=VMEM_LIMIT),
        cost_estimate=cost(count),
    )(pltpu.with_memory_space_constraint(slab, pltpu.HBM), rot)


def raw_kernel(x_ref, p0_ref, p1_ref, p2_ref, p3_ref, _, out_ref, full, rot):
    @pl.when(pl.program_id(0) == 0)
    def _():
        for d, piece in enumerate((p0_ref, p1_ref, p2_ref, p3_ref)):
            core, x, y = place()
            for n in range(8):
                start = ((4 * (y ^ d) + (x ^ (n >> 1))) * 2 + (core ^ (n & 1))) * 8
                full[pl.ds(pl.multiple_of(start, 8), 8), :] = piece[8 * n : 8 * n + 8, :]
        high = full[...].astype(BF16)
        rot[:, 0:128] = high
        rot[:, 128:256] = (full[...] - high.astype(F32)).astype(BF16)

    out_ref[...] = rotation(x_ref[...], rot[...])


def rotated_raw(raw, pieces, result, rows=RAW // PIECES):
    count = raw.shape[0]
    piece = pl.BlockSpec((64, BLOCK), lambda i: (0, 0))
    return pl.pallas_call(
        raw_kernel,
        grid=(count // rows,),
        in_specs=[
            pl.BlockSpec((rows, WIDTH), lambda i: (i, 0)),
            piece,
            piece,
            piece,
            piece,
            pl.BlockSpec(memory_space=pl.ANY),
        ],
        out_specs=pl.BlockSpec((rows, BLOCK), lambda i: (i, 1)),
        out_shape=pltpu.HBM(result.shape, F32),
        scratch_shapes=[pltpu.VMEM((WIDTH, BLOCK), F32), pltpu.VMEM((WIDTH, WIDTH), BF16)],
        input_output_aliases={5: 0},
        compiler_params=pltpu.CompilerParams(vmem_limit_bytes=VMEM_LIMIT),
        cost_estimate=cost(count),
    )(raw, *pieces, result)


def per_device(slab, block_ids):
    core, _, _ = place()
    parts, raw = summed_over_rows(local_gram(slab), core, slab[:RAW])
    first, rot_leave, rot_stay, diag = rounds_and_first_chunk(parts, slab, block_ids)
    first, raw = lax.optimization_barrier((first, raw))
    arrived = [passed_along(first)]
    extra = arrived[0][CHUNKS[0] :]
    starts = [RAW + sum(CHUNKS[:n]) for n in range(len(CHUNKS))]
    for start, count in zip(starts[1:], CHUNKS[1:]):
        arrived.append(passed_along(leaving(slab, rot_leave, start, count)))
    new_slab = staying(slab, rot_stay)
    both = jnp.concatenate([extra[:8], exchanged(extra[:8], 1)])
    eight = jnp.concatenate(with_three_others(both, 1))
    new_slab = rotated_raw(raw, with_three_others(eight, 3), new_slab)
    for start, count, chunk in zip(starts, CHUNKS, arrived):
        new_slab = lax.dynamic_update_slice(new_slab, chunk[:count], (start, BLOCK))
    total_rows = slab.shape[0] * lax.axis_size("row")
    squares = jnp.concatenate([diag[0, :BLOCK], extra[8]])
    col_norms = jnp.sqrt(jnp.maximum(squares, 0.0) / total_rows)
    new_ids = jnp.stack([jnp.min(block_ids), extra[12, 0].astype(jnp.int32)])
    return (new_slab, col_norms, new_ids)


def solution(mesh):
    return jax.shard_map(
        per_device,
        mesh=mesh,
        in_specs=(P("row", "pair"), P("pair")),
        out_specs=(P("row", "pair"), P("pair"), P("pair")),
        check_vma=False,
    )
```
